512 devices in a mesh: doc: 128 (over z, y, core), term: 4 (over x).
Axes of the slice: x: 4, y: 8, z: 8, core: 2. Of those that a mesh axis runs over, the one named last changes fastest.
Arguments:
- tf_blocks: bfloat16 [128, 8192, 512], P('doc', 'term'), as said below
- block_scale: float32 [128, 64, 4], P('doc', 'term'), may hold values from 0.3 to 3
- term_blocks: int32 [128, 64], P('doc', 'term'), may hold values from 0 to 255, as said below
- prior_rows: bfloat16 [128, 8192, 256], P('doc', 'term'), as said below
- prior_sv: float32 [256], replicated, may hold values from 0.3 to 1.5
Outputs:
- doc_coords: float32 [65536, 256], P(('doc', 'term'))
- new_rows: bfloat16 [128, 8192, 256], P('doc', 'term')
- singular: float32 [256], replicated
The draws below stay inside these ranges and needn't reach their ends.
Inputs may be any that keep to these rules, and one draw needn't show every extreme that they name: `term_blocks`: within one batch and one index of term the 16 block ids are distinct and increasing. `prior_rows`: stored rows with the same term row are equal in every batch. `tf_blocks`: entries are nonnegative; about half are zero.
All inputs are finite; a program needn't handle non-finite values.
Results may differ from the reference program's by a relative error of at most 0.0078.
Values sent between devices are 32-bit elements; how exact they have to be, the bound alone decides.
No kernel may reach another device: no remote copies, remote signals or barrier semaphores. Data moves between devices by JAX's collectives and lax.ppermute only.
A program may use at most 64 MiB of HBM per device.

```python
import math
import jax
import jax.numpy as jnp
from jax import lax

K = 256
TERMS = 131072
BLOCK = 128
RB = 16
DOC_BLOCKS = 4
ITERS = 4
TBS = 256
DOCS = 65536
SROWS = 8192
N_DOC = 128
N_TERM = 4


def pick_blocks(key):
    key = jax.random.fold_in(key, 11)
    shard_blocks = TERMS // (BLOCK * N_TERM)
    raw = jax.random.randint(key, (N_DOC, N_TERM, shard_blocks), 0, 1 << 20)
    scores = raw * shard_blocks + jnp.arange(shard_blocks, dtype=jnp.int32)
    scores = scores.at[0, :, shard_blocks - 1].set(-1)
    scores = scores.at[N_DOC - 1, :, 0].set(-1)
    order = jnp.argsort(scores, axis=-1)
    chosen = jnp.sort(order[:, :, :RB], axis=-1)
    return chosen.reshape(N_DOC, N_TERM * RB).astype(jnp.int32)


def draw_term_blocks(key, part):
    return pick_blocks(key)


def draw_prior_rows(key, part):
    block_ids = pick_blocks(key)
    key = jax.random.fold_in(key, 5)
    shard_blocks = TERMS // (BLOCK * N_TERM)
    table = jax.random.normal(key, (TERMS // BLOCK, BLOCK, K), jnp.float32)
    shard_of = jnp.arange(N_TERM * RB, dtype=jnp.int32) // RB
    global_ids = shard_of[None, :] * shard_blocks + block_ids
    picked = table[global_ids]
    return picked.reshape(N_DOC, RB * BLOCK * N_TERM, K).astype(jnp.bfloat16)


def draw_tf_blocks(key, part):
    key = jax.random.fold_in(key, 7)
    keys = jax.random.split(key, 4)
    shape = (N_DOC, RB * BLOCK * N_TERM, DOC_BLOCKS * BLOCK)
    magnitude = jnp.abs(jax.random.normal(keys[0], shape, jnp.float32))
    present = (jax.random.uniform(keys[1], shape, jnp.float32) < 0.5).astype(jnp.float32)
    row_factor = jnp.exp(jax.random.uniform(keys[2], (N_DOC, shape[1], 1), jnp.float32, -1.15, 1.15))
    doc_factor = jnp.exp(jax.random.uniform(keys[3], (N_DOC, 1, shape[2]), jnp.float32, -1.15, 1.15))
    batch_factor = 0.6 + 1.2 * jnp.arange(N_DOC, dtype=jnp.float32) / (N_DOC - 1)
    values = magnitude * present * row_factor * doc_factor * batch_factor[:, None, None]
    return values.astype(jnp.bfloat16)


def steps_of(own_key, dims, pieces, least, high):
    loudness = 1.0
    for position, shards_of in pieces:
        steps = jax.random.uniform(jax.random.fold_in(jax.random.fold_in(own_key, 6), position), (shards_of,), jnp.float32, least / len(pieces), high / len(pieces))
        loudness = loudness * jnp.repeat(jnp.exp(steps), dims[position] // shards_of).reshape((-1,) + (1,) * (len(dims) - 1 - position))
    return loudness


def setup_inputs(seed: int = 0) -> dict:
    seeds = jax.random.split(jax.random.key(seed), 6)
    return {
        "tf_blocks": draw_tf_blocks(jax.random.fold_in(seeds[5], 71), 0),
        "block_scale": jnp.clip(jnp.exp(math.log(3.0) - 2.3025851 * jax.random.uniform(seeds[1], (N_DOC, RB * N_TERM, DOC_BLOCKS), jnp.float32) ** steps_of(seeds[1], (N_DOC, RB * N_TERM, DOC_BLOCKS), ((0, 128), (1, 4)), -0.2, 0.2)), 0.3, 3.0),
        "term_blocks": draw_term_blocks(jax.random.fold_in(seeds[5], 71), 0),
        "prior_rows": draw_prior_rows(jax.random.fold_in(seeds[5], 71), 0),
        "prior_sv": jnp.clip(jnp.exp(jax.random.uniform(seeds[4], (K,), jnp.float32, math.log(0.3), math.log(1.5))), 0.3, 1.5),
    }


forget_factor = 0.85

def orthonormal(matrix):
    lower_one = jnp.linalg.cholesky(jnp.dot(matrix.T, matrix, precision=lax.Precision.HIGHEST))
    return lax.linalg.triangular_solve(lower_one, matrix, left_side=False, lower=True, transpose_a=True)

def reference(tf_blocks, block_scale, term_blocks, prior_rows, prior_sv):
    stored = jnp.arange(SROWS, dtype=jnp.int32)
    shard_of = stored // (RB * BLOCK)
    slot_of = stored // BLOCK
    within = stored % BLOCK
    term_row = shard_of[None, :] * (TBS * BLOCK) + term_blocks[:, slot_of] * BLOCK + within[None, :]
    scale_rows = block_scale[:, slot_of, :]

    def batch_mass(operands):
        counts, scales = operands
        sums = lax.optimization_barrier(jnp.sum(counts.astype(jnp.float32).reshape(SROWS, DOC_BLOCKS, BLOCK), axis=2))
        return lax.optimization_barrier(jnp.sum(sums * scales, axis=1))
    row_mass = lax.map(batch_mass, (tf_blocks, scale_rows))
    term_mass = jax.ops.segment_sum(row_mass.reshape(-1), term_row.reshape(-1).astype(jnp.int32), num_segments=TERMS)
    weight = jnp.log(1.0 + DOCS / (1.0 + term_mass[term_row]))
    root_terms = math.sqrt(TERMS)

    def batch_proj(operands):
        counts, basis_rows, weights, scales = operands
        outputs = []
        for column in range(DOC_BLOCKS):
            factor = weights * scales[:, column] / root_terms
            basis_half = (basis_rows.astype(jnp.float32) * factor[:, None]).astype(jnp.bfloat16)
            doc_block = counts[:, column * BLOCK:(column + 1) * BLOCK]
            outputs.append(jnp.dot(doc_block.T.astype(jnp.float32), basis_half.astype(jnp.float32), preferred_element_type=jnp.float32))
        return jnp.concatenate(outputs, axis=0)
    proj = lax.map(batch_proj, (tf_blocks, prior_rows, weight, scale_rows)).reshape(DOCS, K)
    gram = jnp.dot(proj.T, proj, precision=lax.Precision.HIGHEST) / DOCS + jnp.diag(forget_factor * prior_sv * prior_sv)
    lower = jnp.linalg.cholesky(gram)
    rotation = jnp.eye(K, dtype=jnp.float32)
    for iteration in range(ITERS):
        inner = jnp.dot(lower.T, rotation, precision=lax.Precision.HIGHEST)
        rotation = orthonormal(jnp.dot(lower, inner, precision=lax.Precision.HIGHEST))
    singular = jnp.sqrt(lax.optimization_barrier(jnp.sum(jnp.square(jnp.dot(lower.T, rotation, precision=lax.Precision.HIGHEST)), axis=0)))
    doc_coords = jnp.dot(proj, rotation, precision=lax.Precision.HIGHEST)
    rotation_half = rotation.astype(jnp.bfloat16)

    def rotate_rows(basis_rows):
        return jnp.dot(basis_rows.astype(jnp.float32), rotation_half.astype(jnp.float32), preferred_element_type=jnp.float32).astype(jnp.bfloat16)
    new_rows = lax.map(rotate_rows, prior_rows)
    return (doc_coords, new_rows, singular)
```

```python
import math

import jax
import jax.numpy as jnp
from jax import lax
from jax.sharding import PartitionSpec as P

TERMS = 131072
ITERS = 4
SHARE_BLOCKS = 256


forget_factor = 0.85
highest = lax.Precision.HIGHEST


def orthonormal(matrix):
    lower_one = jnp.linalg.cholesky(jnp.dot(matrix.T, matrix, precision=highest))
    return lax.linalg.triangular_solve(
        lower_one, matrix, left_side=False, lower=True, transpose_a=True
    )


def sum_scatter(pieces, axes):
    return jnp.sum(lax.all_to_all(pieces, axes, 0, 0, tiled=True), axis=0)


def gather(piece, axes, count):
    repeated = jnp.broadcast_to(piece[None], (count,) + piece.shape)
    return lax.all_to_all(repeated, axes, 0, 0, tiled=True)


def shards(tf_blocks, block_scale, term_blocks, prior_rows, prior_sv):
    counts = tf_blocks[0]
    scales = block_scale[0]
    block_ids = term_blocks[0]
    basis_rows = prior_rows[0]
    stored_blocks = block_ids.shape[0]
    height = counts.shape[0]
    block_width = height // stored_blocks
    batch_docs = counts.shape[1]
    doc_blocks = batch_docs // block_width
    rank_size = basis_rows.shape[1]
    doc_count = lax.axis_size("doc")
    term_count = lax.axis_size("term")
    total_docs = batch_docs * doc_count
    share_docs = batch_docs // term_count
    marker = (
        jnp.arange(batch_docs, dtype=jnp.int32)[:, None] // block_width
        == jnp.arange(doc_blocks, dtype=jnp.int32)[None, :]
    ).astype(jnp.bfloat16)
    block_sums = jnp.dot(counts, marker, preferred_element_type=jnp.float32)
    scale_rows = jnp.repeat(scales, block_width, axis=0)
    row_mass = jnp.sum(block_sums * scale_rows, axis=1).reshape(stored_blocks, block_width)
    places = (
        block_ids[:, None] == jnp.arange(SHARE_BLOCKS, dtype=jnp.int32)[None, :]
    ).astype(jnp.float32)
    dense = jnp.dot(places.T, row_mass, precision=highest)
    dense_pieces = dense.reshape(doc_count, SHARE_BLOCKS // doc_count, block_width)
    own_mass = sum_scatter(dense_pieces, "doc")
    share_mass = gather(own_mass, "doc", doc_count).reshape(SHARE_BLOCKS, block_width)
    term_mass = jnp.dot(places, share_mass, precision=highest)
    weight = jnp.log(1.0 + total_docs / (1.0 + term_mass)).reshape(height)
    root_terms = math.sqrt(TERMS)
    pieces = []
    for column in range(doc_blocks):
        basis_half = (
            basis_rows * (weight * scale_rows[:, column] / root_terms)[:, None]
        ).astype(jnp.bfloat16)
        doc_block = counts[:, column * block_width : (column + 1) * block_width]
        pieces.append(
            lax.dot_general(
                doc_block, basis_half, (((0,), (0,)), ((), ())), preferred_element_type=jnp.float32
            )
        )
    partial = jnp.concatenate(pieces, axis=0).reshape(term_count, share_docs, rank_size)
    share_rows = sum_scatter(partial, "term")
    own_gram = jnp.dot(share_rows.T, share_rows, precision=highest) / total_docs
    everyone = ("doc", "term")
    device_count = doc_count * term_count
    gram_pieces = own_gram.reshape(device_count, 1, rank_size * rank_size // device_count)
    gram_piece = sum_scatter(gram_pieces, everyone)
    window = gather(gram_piece, everyone, device_count).reshape(rank_size, rank_size)
    gram = window + jnp.diag(forget_factor * prior_sv * prior_sv)
    rotation = orthonormal(gram)
    for iteration in range(ITERS - 1):
        rotation = orthonormal(jnp.dot(gram, rotation, precision=highest))
    singular = jnp.sqrt(
        jnp.sum(rotation * jnp.dot(gram, rotation, precision=highest), axis=0)
    )
    doc_coords = jnp.dot(share_rows, rotation, precision=highest)
    rotation_half = rotation.astype(jnp.bfloat16)
    new_rows = jnp.dot(basis_rows, rotation_half, preferred_element_type=jnp.float32).astype(
        jnp.bfloat16
    )
    return (doc_coords, new_rows[None], singular)


def solution(mesh):
    in_specs = (
        P("doc", "term", None),
        P("doc", "term", None),
        P("doc", "term"),
        P("doc", "term", None),
        P(),
    )
    out_specs = (P(("doc", "term"), None), P("doc", "term", None), P())
    return jax.shard_map(shards, mesh=mesh, in_specs=in_specs, out_specs=out_specs, check_vma=False)
```

```python
import functools
import math

import jax
import jax.numpy as jnp
from jax import lax
from jax.experimental import pallas as pl
from jax.experimental.pallas import tpu as pltpu
from jax.sharding import Mesh
from jax.sharding import PartitionSpec as P

TERMS = 131072
ITERS = 4
SHARE_BLOCKS = 256
LANES = 128
PANEL = 16
OUTER = 128


forget_factor = 0.85
highest = lax.Precision.HIGHEST


def contract(a, b, a_dim, b_dim):
    return lax.dot_general(
        a,
        b,
        (((a_dim,), (b_dim,)), ((), ())),
        precision=highest,
        preferred_element_type=jnp.float32,
    )


def eliminate(panel, first):
    size = panel.shape[0]
    rows = lax.broadcasted_iota(jnp.int32, (size, LANES), 0)
    columns = [
        jnp.broadcast_to(panel[:, first + k : first + k + 1], (size, LANES)) for k in range(size)
    ]
    tiles = [panel[:, t : t + LANES] for t in range(0, panel.shape[1], LANES)]
    pivots = jnp.zeros((size, LANES), jnp.float32)
    for k in range(size):
        pivot = columns[k][k : k + 1, :]
        pivots = jnp.where(rows == k, jnp.broadcast_to(pivot, (size, LANES)), pivots)
        if k + 1 < size:
            factor = jnp.where(rows > k, columns[k] * (1.0 / pivot), 0.0)
            for m in range(k + 1, size):
                columns[m] = columns[m] - factor * columns[m][k : k + 1, :]
            tiles = [tile - factor * tile[k : k + 1, :] for tile in tiles]
    root = lax.rsqrt(pivots)
    return jnp.concatenate([tile * root for tile in tiles], axis=1)


def orthonormal_rows(work):
    size = work.shape[0]
    for outer in range(0, size, OUTER):
        end = outer + OUTER
        for first in range(outer, end, PANEL):
            panel = work[first : first + PANEL, :]
            if first > outer:
                panel = panel - contract(
                    work[outer:first, first : first + PANEL], work[outer:first, :], 0, 0
                )
            work[first : first + PANEL, :] = eliminate(panel, first)
        if end < size:
            work[end:, :] = work[end:, :] - contract(work[outer:end, end:size], work[outer:end, :], 0, 0)


def iterate(window_ref, sv_ref, rotation_ref, singular_ref, gram, work):
    size = window_ref.shape[0]
    row = lax.broadcasted_iota(jnp.int32, (size, size), 0)
    column = lax.broadcasted_iota(jnp.int32, (size, size), 1)
    sv = sv_ref[...]
    gram[...] = window_ref[...] + jnp.where(row == column, forget_factor * sv * sv, 0.0)
    work[:, size:] = gram[...]

    def step(iteration, carry):
        image = work[:, size:]
        work[:, :size] = contract(image, image, 1, 1)
        orthonormal_rows(work)
        rotation_ref[...] = work[:, size:]
        work[:, size:] = contract(rotation_ref[...], gram[...], 1, 0)
        return carry

    lax.fori_loop(0, ITERS, step, 0)
    singular_ref[...] = jnp.sqrt(
        jnp.sum(rotation_ref[...] * work[:, size:], axis=1, keepdims=True)
    )


def all_to_all(pieces, axes):
    return lax.all_to_all(pieces, axes, 0, 0, tiled=True)


def repeat(piece, count):
    return jnp.broadcast_to(piece[None], (count,) + piece.shape)


def swap_cores(array):
    return lax.ppermute(array, "core", [(0, 1), (1, 0)])


def split_cores(array):
    half = array.shape[0] // 2
    first = lax.axis_index("core") == 0
    low, high = array[:half], array[half:]
    return jnp.where(first, low, high) + swap_cores(jnp.where(first, high, low))


def join_cores(half):
    other = swap_cores(half)
    first = lax.axis_index("core") == 0
    return jnp.concatenate([jnp.where(first, half, other), jnp.where(first, other, half)], axis=0)


def shards(tf_blocks, block_scale, term_blocks, prior_rows, prior_sv):
    counts = tf_blocks[0]
    scales = block_scale[0]
    block_ids = term_blocks[0]
    basis_rows = prior_rows[0]
    stored_blocks = block_ids.shape[0]
    height = counts.shape[0]
    block_width = height // stored_blocks
    batch_docs = counts.shape[1]
    doc_blocks = batch_docs // block_width
    rank_size = basis_rows.shape[1]
    planes, lines = lax.axis_size("z"), lax.axis_size("y")
    doc_count = planes * lines * lax.axis_size("core")
    term_count = lax.axis_size("term")
    total_docs = batch_docs * doc_count
    share_docs = batch_docs // term_count
    marker = (
        jnp.arange(batch_docs, dtype=jnp.int32)[:, None] // block_width
        == jnp.arange(doc_blocks, dtype=jnp.int32)[None, :]
    ).astype(jnp.bfloat16)
    block_sums = jnp.dot(counts, marker, preferred_element_type=jnp.float32)
    scale_rows = jnp.repeat(scales, block_width, axis=0)
    row_mass = jnp.sum(block_sums * scale_rows, axis=1).reshape(stored_blocks, block_width)
    places = (
        block_ids[:, None] == jnp.arange(SHARE_BLOCKS, dtype=jnp.int32)[None, :]
    ).astype(jnp.float32)
    dense = jnp.dot(places.T, row_mass, precision=highest)
    chips = ("z", "y")
    chip_count = planes * lines
    half_mass = split_cores(dense).reshape(chip_count, -1, block_width)
    own_mass = jnp.sum(all_to_all(half_mass, chips), axis=0)
    half_mass = all_to_all(repeat(own_mass, chip_count), chips).reshape(-1, block_width)
    share_mass = join_cores(half_mass)
    term_mass = jnp.dot(places, share_mass, precision=highest)
    weight = jnp.log(1.0 + total_docs / (1.0 + term_mass)).reshape(height)
    root_terms = math.sqrt(TERMS)
    pieces = []
    for column in range(doc_blocks):
        basis_half = (
            basis_rows * (weight * scale_rows[:, column] / root_terms)[:, None]
        ).astype(jnp.bfloat16)
        doc_block = counts[:, column * block_width : (column + 1) * block_width]
        pieces.append(
            lax.dot_general(
                doc_block, basis_half, (((0,), (0,)), ((), ())), preferred_element_type=jnp.float32
            )
        )
    partial = jnp.concatenate(pieces, axis=0).reshape(term_count, share_docs, rank_size)
    share_rows = jnp.sum(all_to_all(partial, "term"), axis=0)
    own_gram = jnp.dot(share_rows.T, share_rows, precision=highest) / total_docs
    flat_gram = jnp.concatenate([own_gram[:, t : t + LANES] for t in range(0, rank_size, LANES)])
    plane = ("y", "term")
    plane_count = lines * term_count
    half_gram = split_cores(flat_gram).reshape(plane_count, -1, LANES)
    plane_gram = jnp.sum(all_to_all(half_gram, plane), axis=0)
    piece_gram = jnp.sum(all_to_all(repeat(plane_gram, planes), "z"), axis=0)
    half_gram = all_to_all(repeat(piece_gram, plane_count), plane).reshape(-1, LANES)
    flat_gram = join_cores(half_gram)
    window = jnp.concatenate(
        [flat_gram[t : t + rank_size] for t in range(0, flat_gram.shape[0], rank_size)], axis=1
    )
    rotation, singular = pl.pallas_call(
        iterate,
        out_shape=(
            jax.ShapeDtypeStruct((rank_size, rank_size), jnp.float32),
            jax.ShapeDtypeStruct((rank_size, 1), jnp.float32),
        ),
        scratch_shapes=[
            pltpu.VMEM((rank_size, rank_size), jnp.float32),
            pltpu.VMEM((rank_size, 2 * rank_size), jnp.float32),
        ],
        compiler_params=pltpu.CompilerParams(vmem_limit_bytes=32 * 2**20),
    )(window, prior_sv.reshape(1, rank_size))
    doc_coords = contract(share_rows, rotation, 1, 1)
    rotation_half = rotation.astype(jnp.bfloat16)
    new_rows = lax.dot_general(
        basis_rows, rotation_half, (((1,), (1,)), ((), ())), preferred_element_type=jnp.float32
    ).astype(jnp.bfloat16)
    return (doc_coords, new_rows[None], singular.reshape(rank_size))


def solution(mesh):
    planes = lines = 8
    named = Mesh(
        mesh.devices.reshape(planes, lines, -1, mesh.shape["term"]), ("z", "y", "core", "term")
    )
    doc = ("z", "y", "core")
    in_specs = (
        P(doc, "term", None),
        P(doc, "term", None),
        P(doc, "term"),
        P(doc, "term", None),
        P(),
    )
    out_specs = (P(doc + ("term",), None), P(doc, "term", None), P())
    return jax.shard_map(shards, mesh=named, in_specs=in_specs, out_specs=out_specs, check_vma=False)
```

```python
import math

import jax
import jax.numpy as jnp
from jax import lax
from jax.experimental import pallas as pl
from jax.experimental.pallas import tpu as pltpu
from jax.sharding import Mesh
from jax.sharding import PartitionSpec as P

TERMS = 131072
ITERS = 4
LANES = 128
PANEL = 16
OUTER = 128


forget_factor = 0.85
highest = lax.Precision.HIGHEST


def contract(a, b, a_dim, b_dim):
    return lax.dot_general(
        a,
        b,
        (((a_dim,), (b_dim,)), ((), ())),
        precision=highest,
        preferred_element_type=jnp.float32,
    )


def eliminate(panel, first):
    size = panel.shape[0]
    rows = lax.broadcasted_iota(jnp.int32, (size, LANES), 0)
    columns = [
        jnp.broadcast_to(panel[:, first + k : first + k + 1], (size, LANES)) for k in range(size)
    ]
    tiles = [panel[:, t : t + LANES] for t in range(0, panel.shape[1], LANES)]
    pivots = jnp.zeros((size, LANES), jnp.float32)
    for k in range(size):
        pivot = columns[k][k : k + 1, :]
        pivots = jnp.where(rows == k, jnp.broadcast_to(pivot, (size, LANES)), pivots)
        if k + 1 < size:
            factor = jnp.where(rows > k, columns[k] * (1.0 / pivot), 0.0)
            for m in range(k + 1, size):
                columns[m] = columns[m] - factor * columns[m][k : k + 1, :]
            tiles = [tile - factor * tile[k : k + 1, :] for tile in tiles]
    root = lax.rsqrt(pivots)
    return jnp.concatenate([tile * root for tile in tiles], axis=1)


def orthonormal_rows(work):
    size = work.shape[0]
    for outer in range(0, size, OUTER):
        end = outer + OUTER
        for first in range(outer, end, PANEL):
            panel = work[first : first + PANEL, :]
            if first > outer:
                panel = panel - contract(
                    work[outer:first, first : first + PANEL], work[outer:first, :], 0, 0
                )
            work[first : first + PANEL, :] = eliminate(panel, first)
        if end < size:
            work[end:, :] = work[end:, :] - contract(work[outer:end, end:size], work[outer:end, :], 0, 0)


def normalise(work):
    size = work.shape[0]
    image = work[:, size:]
    work[:, :size] = contract(image, image, 1, 1)
    orthonormal_rows(work)


def rotate(
    window_ref, sv_ref, share_ref, prior_hbm,
    coords_ref, rows_hbm, singular_ref,
    gram, work, rotation, prior, rows, load, store,
):
    loading = pltpu.make_async_copy(prior_hbm, prior, load)
    loading.start()
    size = window_ref.shape[0]
    row = lax.broadcasted_iota(jnp.int32, (size, size), 0)
    column = lax.broadcasted_iota(jnp.int32, (size, size), 1)
    sv = sv_ref[...]
    whole = window_ref[...] + jnp.where(row == column, forget_factor * sv * sv, 0.0)
    gram[...] = whole
    diagonal = jnp.where(row == column, whole, 0.0)
    top = jnp.max(jnp.max(diagonal, axis=0, keepdims=True), axis=1, keepdims=True)
    scaled = whole * (1.0 / top)
    square = contract(scaled, scaled, 1, 0)
    work[:, size:] = contract(square, square, 1, 0)
    normalise(work)
    result = work[:, size:]
    miss = contract(result, result, 1, 1) - jnp.where(row == column, 1.0, 0.0)
    half = jnp.where(row > column, miss, jnp.where(row == column, 0.5 * miss, 0.0))
    rotation[...] = result - contract(half, result, 1, 0)
    sound = jnp.sum(miss * miss) < 1e-2

    @pl.when(jnp.logical_not(sound))
    def _():
        work[:, size:] = gram[...]

        def step(iteration, carry):
            normalise(work)
            rotation[...] = work[:, size:]
            work[:, size:] = contract(rotation[...], gram[...], 1, 0)
            return carry

        lax.fori_loop(0, ITERS, step, 0)

    turned = rotation[...]
    turned_half = turned.astype(jnp.bfloat16)
    loading.wait()
    parts = store.shape[0]
    height = rows.shape[0] // parts
    storing = []
    for part in range(parts):
        span = pl.ds(part * height, height)
        rows[span, :] = lax.dot_general(
            prior[span, :], turned_half, (((1,), (1,)), ((), ())), preferred_element_type=jnp.float32
        ).astype(jnp.bfloat16)
        copy = pltpu.make_async_copy(rows.at[span], rows_hbm.at[span], store.at[part])
        copy.start()
        storing.append(copy)
    coords_ref[...] = contract(share_ref[...], turned, 1, 1)
    energy = turned * contract(turned, gram[...], 1, 0)
    total = contract(jnp.ones((8, size), jnp.float32), energy, 1, 1)
    singular_ref[...] = jnp.sqrt(total[:1])
    for copy in storing:
        copy.wait()


def all_to_all(pieces, axes):
    return lax.all_to_all(pieces, axes, 0, 0, tiled=True)


def repeat(piece, count):
    return jnp.broadcast_to(piece[None], (count,) + piece.shape)


def swap_cores(array):
    return lax.ppermute(array, "core", [(0, 1), (1, 0)])


def finish(window, prior_sv, share_rows, basis_rows):
    height, rank_size = basis_rows.shape
    parts = 4
    return pl.pallas_call(
        rotate,
        in_specs=[pl.BlockSpec(memory_space=pltpu.VMEM)] * 3 + [pl.BlockSpec(memory_space=pl.ANY)],
        out_specs=(
            pl.BlockSpec(memory_space=pltpu.VMEM),
            pl.BlockSpec(memory_space=pl.ANY),
            pl.BlockSpec(memory_space=pltpu.VMEM),
        ),
        out_shape=(
            jax.ShapeDtypeStruct(share_rows.shape, jnp.float32),
            jax.ShapeDtypeStruct((height, rank_size), jnp.bfloat16),
            jax.ShapeDtypeStruct((1, rank_size), jnp.float32),
        ),
        scratch_shapes=[
            pltpu.VMEM((rank_size, rank_size), jnp.float32),
            pltpu.VMEM((rank_size, 2 * rank_size), jnp.float32),
            pltpu.VMEM((rank_size, rank_size), jnp.float32),
            pltpu.VMEM((height, rank_size), jnp.bfloat16),
            pltpu.VMEM((height, rank_size), jnp.bfloat16),
            pltpu.SemaphoreType.DMA,
            pltpu.SemaphoreType.DMA((parts,)),
        ],
        compiler_params=pltpu.CompilerParams(vmem_limit_bytes=32 * 2**20),
    )(window, prior_sv.reshape(1, rank_size), share_rows, basis_rows)


def shards(tf_blocks, block_scale, term_blocks, prior_rows, prior_sv):
    counts = tf_blocks[0]
    scales = block_scale[0]
    block_ids = term_blocks[0]
    basis_rows = prior_rows[0]
    stored_blocks = block_ids.shape[0]
    height = counts.shape[0]
    block_width = height // stored_blocks
    batch_docs = counts.shape[1]
    doc_blocks = batch_docs // block_width
    rank_size = basis_rows.shape[1]
    planes, lines = lax.axis_size("z"), lax.axis_size("y")
    doc_count = planes * lines * lax.axis_size("core")
    term_count = lax.axis_size("term")
    total_docs = batch_docs * doc_count
    share_docs = batch_docs // term_count
    marker = (
        jnp.arange(batch_docs, dtype=jnp.int32)[:, None] // block_width
        == jnp.arange(doc_blocks, dtype=jnp.int32)[None, :]
    ).astype(jnp.bfloat16)
    block_sums = jnp.dot(counts, marker, preferred_element_type=jnp.float32)
    scale_rows = jnp.repeat(scales, block_width, axis=0)
    row_mass = jnp.sum(block_sums * scale_rows, axis=1).reshape(stored_blocks, block_width)
    half_width = block_width // 2
    id_values = block_ids.astype(jnp.float32)
    tail = jnp.pad(id_values, (0, LANES - stored_blocks))
    halves = jnp.stack(
        [
            jnp.concatenate([row_mass[:, side : side + half_width].reshape(-1), tail])
            for side in (0, half_width)
        ]
    )
    outgoing = jnp.broadcast_to(halves[None], (doc_count // 2,) + halves.shape)
    incoming = all_to_all(outgoing.reshape(doc_count, 1, -1), ("z", "y", "core"))
    incoming = incoming.reshape(doc_count, -1, LANES)
    slots = LANES // half_width
    slot_rows = stored_blocks // slots
    masses = incoming[:, :slot_rows].reshape(doc_count * slot_rows, LANES)
    all_ids = incoming[:, slot_rows, :stored_blocks]
    chip = lax.axis_index("z") * lines + lax.axis_index("y")
    pair_ids = lax.dynamic_slice_in_dim(all_ids, 2 * chip, 2, 0).reshape(-1)
    pair_mass = 0.0
    for slot in range(slots):
        slot_ids = all_ids[:, slot::slots].reshape(-1)
        matches = (pair_ids[:, None] == slot_ids[None, :]).astype(jnp.float32)
        found = jnp.dot(matches, masses, precision=highest)
        pair_mass = pair_mass + found[:, slot * half_width : (slot + 1) * half_width]
    first = lax.axis_index("core") == 0
    low, high = pair_mass[:stored_blocks], pair_mass[stored_blocks:]
    mine = jnp.where(first, low, high)
    other = swap_cores(jnp.where(first, high, low))
    term_mass = jnp.concatenate(
        [jnp.where(first, mine, other), jnp.where(first, other, mine)], axis=1
    )
    weight = jnp.log(1.0 + total_docs / (1.0 + term_mass)).reshape(height)
    root_terms = math.sqrt(TERMS)
    pieces = []
    for column in range(doc_blocks):
        basis_half = (
            basis_rows * (weight * scale_rows[:, column] / root_terms)[:, None]
        ).astype(jnp.bfloat16)
        doc_block = counts[:, column * block_width : (column + 1) * block_width]
        pieces.append(
            lax.dot_general(
                doc_block, basis_half, (((0,), (0,)), ((), ())), preferred_element_type=jnp.float32
            )
        )
    partial = jnp.concatenate(pieces, axis=0).reshape(term_count, share_docs, rank_size)
    share_rows = jnp.sum(all_to_all(partial, "term"), axis=0)
    own_gram = jnp.dot(share_rows.T, share_rows, precision=highest) / total_docs
    flat_gram = jnp.concatenate([own_gram[:, t : t + LANES] for t in range(0, rank_size, LANES)])
    plane = ("y", "term")
    across = ("z", "core")
    plane_count = lines * term_count
    plane_gram = jnp.sum(all_to_all(flat_gram.reshape(plane_count, -1, LANES), plane), axis=0)
    piece_gram = jnp.sum(all_to_all(repeat(plane_gram, doc_count // lines), across), axis=0)
    flat_gram = all_to_all(repeat(piece_gram, plane_count), plane).reshape(-1, LANES)
    window = jnp.concatenate(
        [flat_gram[t : t + rank_size] for t in range(0, flat_gram.shape[0], rank_size)], axis=1
    )
    doc_coords, new_rows, singular = finish(window, prior_sv, share_rows, basis_rows)
    return (doc_coords, new_rows[None], singular.reshape(rank_size))


def solution(mesh):
    planes = lines = 8
    named = Mesh(
        mesh.devices.reshape(planes, lines, -1, mesh.shape["term"]), ("z", "y", "core", "term")
    )
    doc = ("z", "y", "core")
    in_specs = (
        P(doc, "term", None),
        P(doc, "term", None),
        P(doc, "term"),
        P(doc, "term", None),
        P(),
    )
    out_specs = (P(doc + ("term",), None), P(doc, "term", None), P())
    return jax.shard_map(shards, mesh=named, in_specs=in_specs, out_specs=out_specs, check_vma=False)
```

```python
import functools
import math

import jax
import jax.numpy as jnp
from jax import lax
from jax.experimental import pallas as pl
from jax.experimental.pallas import tpu as pltpu
from jax.sharding import Mesh
from jax.sharding import PartitionSpec as P

TERMS = 131072
ITERS = 4
LANES = 128
PANEL = 16
OUTER = 128


forget_factor = 0.85
highest = lax.Precision.HIGHEST


def contract(a, b, a_dim, b_dim):
    return lax.dot_general(
        a,
        b,
        (((a_dim,), (b_dim,)), ((), ())),
        precision=highest,
        preferred_element_type=jnp.float32,
    )


def eliminate(panel, first):
    size = panel.shape[0]
    rows = lax.broadcasted_iota(jnp.int32, (size, LANES), 0)
    columns = [
        jnp.broadcast_to(panel[:, first + k : first + k + 1], (size, LANES)) for k in range(size)
    ]
    tiles = [panel[:, t : t + LANES] for t in range(0, panel.shape[1], LANES)]
    pivots = jnp.zeros((size, LANES), jnp.float32)
    for k in range(size):
        pivot = columns[k][k : k + 1, :]
        pivots = jnp.where(rows == k, jnp.broadcast_to(pivot, (size, LANES)), pivots)
        if k + 1 < size:
            factor = jnp.where(rows > k, columns[k] * (1.0 / pivot), 0.0)
            for m in range(k + 1, size):
                columns[m] = columns[m] - factor * columns[m][k : k + 1, :]
            tiles = [tile - factor * tile[k : k + 1, :] for tile in tiles]
    root = lax.rsqrt(pivots)
    return jnp.concatenate([tile * root for tile in tiles], axis=1)


def orthonormal_rows(work):
    size = work.shape[0]
    for outer in range(0, size, OUTER):
        end = outer + OUTER
        for first in range(outer, end, PANEL):
            panel = work[first : first + PANEL, :]
            if first > outer:
                panel = panel - contract(
                    work[outer:first, first : first + PANEL], work[outer:first, :], 0, 0
                )
            work[first : first + PANEL, :] = eliminate(panel, first)
        if end < size:
            work[end:, :] = work[end:, :] - contract(work[outer:end, end:size], work[outer:end, :], 0, 0)


def normalise(work):
    size = work.shape[0]
    image = work[:, size:]
    work[:, :size] = contract(image, image, 1, 1)
    orthonormal_rows(work)


def rotate(
    window_ref, sv_ref, share_ref, prior_hbm,
    coords_ref, rows_hbm, singular_ref,
    gram, work, rotation, prior, rows, load, store,
):
    loading = pltpu.make_async_copy(prior_hbm, prior, load)
    loading.start()
    size = window_ref.shape[0]
    row = lax.broadcasted_iota(jnp.int32, (size, size), 0)
    column = lax.broadcasted_iota(jnp.int32, (size, size), 1)
    sv = sv_ref[...]
    whole = window_ref[...] + jnp.where(row == column, forget_factor * sv * sv, 0.0)
    gram[...] = whole
    diagonal = jnp.where(row == column, whole, 0.0)
    top = jnp.max(jnp.max(diagonal, axis=0, keepdims=True), axis=1, keepdims=True)
    scaled = whole * (1.0 / top)
    square = contract(scaled, scaled, 1, 0)
    work[:, size:] = contract(square, square, 1, 0)
    normalise(work)
    result = work[:, size:]
    miss = contract(result, result, 1, 1) - jnp.where(row == column, 1.0, 0.0)
    half = jnp.where(row > column, miss, jnp.where(row == column, 0.5 * miss, 0.0))
    rotation[...] = result - contract(half, result, 1, 0)
    sound = jnp.sum(miss * miss) < 1e-2

    @pl.when(jnp.logical_not(sound))
    def _():
        work[:, size:] = gram[...]

        def step(iteration, carry):
            normalise(work)
            rotation[...] = work[:, size:]
            work[:, size:] = contract(rotation[...], gram[...], 1, 0)
            return carry

        lax.fori_loop(0, ITERS, step, 0)

    turned = rotation[...]
    turned_half = turned.astype(jnp.bfloat16)
    loading.wait()
    parts = store.shape[0]
    height = rows.shape[0] // parts
    storing = []
    for part in range(parts):
        span = pl.ds(part * height, height)
        rows[span, :] = lax.dot_general(
            prior[span, :], turned_half, (((1,), (1,)), ((), ())), preferred_element_type=jnp.float32
        ).astype(jnp.bfloat16)
        copy = pltpu.make_async_copy(rows.at[span], rows_hbm.at[span], store.at[part])
        copy.start()
        storing.append(copy)
    coords_ref[...] = contract(share_ref[...], turned, 1, 1)
    energy = turned * contract(turned, gram[...], 1, 0)
    total = contract(jnp.ones((8, size), jnp.float32), energy, 1, 1)
    singular_ref[...] = jnp.sqrt(total[:1])
    for copy in storing:
        copy.wait()


def all_to_all(pieces, axes):
    return lax.all_to_all(pieces, axes, 0, 0, tiled=True)


def repeat(piece, count):
    return jnp.broadcast_to(piece[None], (count,) + piece.shape)


def swap_cores(array):
    return lax.ppermute(array, "core", [(0, 1), (1, 0)])


def finish(window, prior_sv, share_rows, basis_rows):
    height, rank_size = basis_rows.shape
    parts = 4
    return pl.pallas_call(
        rotate,
        in_specs=[pl.BlockSpec(memory_space=pltpu.VMEM)] * 3 + [pl.BlockSpec(memory_space=pl.ANY)],
        out_specs=(
            pl.BlockSpec(memory_space=pltpu.VMEM),
            pl.BlockSpec(memory_space=pl.ANY),
            pl.BlockSpec(memory_space=pltpu.VMEM),
        ),
        out_shape=(
            jax.ShapeDtypeStruct(share_rows.shape, jnp.float32),
            jax.ShapeDtypeStruct((height, rank_size), jnp.bfloat16),
            jax.ShapeDtypeStruct((1, rank_size), jnp.float32),
        ),
        scratch_shapes=[
            pltpu.VMEM((rank_size, rank_size), jnp.float32),
            pltpu.VMEM((rank_size, 2 * rank_size), jnp.float32),
            pltpu.VMEM((rank_size, rank_size), jnp.float32),
            pltpu.VMEM((height, rank_size), jnp.bfloat16),
            pltpu.VMEM((height, rank_size), jnp.bfloat16),
            pltpu.SemaphoreType.DMA,
            pltpu.SemaphoreType.DMA((parts,)),
        ],
        compiler_params=pltpu.CompilerParams(vmem_limit_bytes=32 * 2**20),
    )(window, prior_sv.reshape(1, rank_size), share_rows, basis_rows)


def mass_pieces_kernel(slots, counts_ref, scale_ref, ids_ref, pieces_ref, mass):
    step = pl.program_id(0)
    width = counts_ref.shape[0] // slots
    docs = counts_ref.shape[1]
    doc_blocks = scale_ref.shape[0]
    marker = (
        lax.broadcasted_iota(jnp.int32, (16, docs), 1) // (docs // doc_blocks)
        == lax.broadcasted_iota(jnp.int32, (16, docs), 0)
    ).astype(jnp.bfloat16)
    for slot in range(slots):
        block = counts_ref[slot * width : (slot + 1) * width, :]
        sums = lax.dot_general(
            marker, block, (((1,), (1,)), ((), ())), preferred_element_type=jnp.float32
        )
        place = step * slots + slot
        total = sums[0:1] * scale_ref[0, place]
        for j in range(1, doc_blocks):
            total = total + sums[j : j + 1] * scale_ref[j, place]
        mass[pl.ds(place, 1), :] = total

    @pl.when(step == pl.num_programs(0) - 1)
    def _():
        stored = mass.shape[0]
        even = jnp.concatenate([mass[q : q + 1, :] for q in range(0, stored, 2)], axis=0)
        odd = jnp.concatenate([mass[q : q + 1, :] for q in range(1, stored, 2)], axis=0)
        half = LANES // 2
        lower = lax.broadcasted_iota(jnp.int32, even.shape, 1) < half
        near = jnp.where(lower, even, pltpu.roll(odd, half, 1))
        far = jnp.where(lower, pltpu.roll(even, half, 1), odd)
        ids = jnp.concatenate(
            [ids_ref[...].astype(jnp.float32), jnp.full((1, LANES - stored), -1.0, jnp.float32)], axis=1
        )
        period = jnp.concatenate([near, ids, far, ids] * 4, axis=0)
        rows = period.shape[0]
        for part in range(pieces_ref.shape[0] // rows):
            pieces_ref[part * rows : (part + 1) * rows, :] = period


def mass_pieces(counts, scales, block_ids, doc_count):
    height, docs = counts.shape
    stored = block_ids.shape[0]
    steps = 4
    return pl.pallas_call(
        functools.partial(mass_pieces_kernel, stored // steps),
        grid=(steps,),
        in_specs=[
            pl.BlockSpec((height // steps, docs), lambda i: (i, 0)),
            pl.BlockSpec(memory_space=pltpu.SMEM),
            pl.BlockSpec((1, stored), lambda i: (0, 0)),
        ],
        out_specs=pl.BlockSpec((doc_count * (stored // 2 + 1), LANES), lambda i: (0, 0)),
        out_shape=jax.ShapeDtypeStruct((doc_count * (stored // 2 + 1), LANES), jnp.float32),
        scratch_shapes=[pltpu.VMEM((stored, height // stored), jnp.float32)],
        compiler_params=pltpu.CompilerParams(vmem_limit_bytes=56 * 2**20),
    )(counts, scales.T, block_ids.reshape(1, stored))


def find_masses_kernel(stored, place_ref, incoming_ref, keep_ref, send_ref):
    piece = stored // 2 + 1
    batches = incoming_ref.shape[0] // piece
    half = LANES // 2
    chip, core = place_ref[0], place_ref[1]
    ids = incoming_ref[pl.ds(piece - 1, batches, stride=piece), :].T[:stored]
    batch = lax.broadcasted_iota(jnp.int32, ids.shape, 1)
    pair = [
        jnp.sum(jnp.where(batch == 2 * chip + side, ids, 0.0), axis=1, keepdims=True)
        for side in (0, 1)
    ]
    wanted = jnp.broadcast_to(jnp.concatenate(pair, axis=0), (2 * stored, batches))
    matches, parts = [], [[], [], []]
    for row in range(piece - 1):
        masses = incoming_ref[pl.ds(row, batches, stride=piece), :]
        high = masses.astype(jnp.bfloat16)
        rest = masses - high.astype(jnp.float32)
        low = rest.astype(jnp.bfloat16)
        last = (rest - low.astype(jnp.float32)).astype(jnp.bfloat16)
        for part, value in zip(parts, (high, low, last)):
            part.append(value)
        match = [
            jnp.where(wanted == ids[2 * row + slot : 2 * row + slot + 1], 1.0, 0.0)
            for slot in range(2)
        ]
        matches.append(jnp.concatenate(match, axis=0).astype(jnp.bfloat16))
    matches = jnp.concatenate(matches, axis=1)
    found = 0.0
    for part in parts:
        found = found + jnp.dot(
            matches, jnp.concatenate(part, axis=0), preferred_element_type=jnp.float32
        )
    masses = found[: 2 * stored, :half] + found[2 * stored :, half:]
    mine = core == 0
    keep_ref[...] = jnp.where(mine, masses[:stored], masses[stored:])
    send_ref[...] = jnp.where(mine, masses[stored:], masses[:stored])


def find_masses(incoming, chip, core, stored):
    shape = jax.ShapeDtypeStruct((stored, LANES // 2), jnp.float32)
    return pl.pallas_call(
        functools.partial(find_masses_kernel, stored),
        in_specs=[
            pl.BlockSpec(memory_space=pltpu.SMEM),
            pl.BlockSpec(memory_space=pltpu.VMEM),
        ],
        out_specs=(pl.BlockSpec(memory_space=pltpu.VMEM), pl.BlockSpec(memory_space=pltpu.VMEM)),
        out_shape=(shape, shape),
        compiler_params=pltpu.CompilerParams(vmem_limit_bytes=16 * 2**20),
    )(jnp.stack([chip, core]).astype(jnp.int32), incoming)


def project_kernel(
    total_docs, core_ref, keep_ref, come_ref, scale_ref, prior_ref, turned_ref, partial_ref, basis
):
    stored = keep_ref.shape[0]
    doc_blocks = scale_ref.shape[0]
    height = prior_ref.shape[0]
    width = height // stored
    docs = partial_ref.shape[0] // doc_blocks
    mine, other = keep_ref[...], come_ref[...]
    first = core_ref[0] == 0
    term_mass = jnp.concatenate(
        [jnp.where(first, mine, other), jnp.where(first, other, mine)], axis=1
    )
    weight = jnp.log(1.0 + total_docs / (1.0 + term_mass))
    spare = jnp.zeros((LANES - stored, LANES), jnp.float32)
    turned_weight = jnp.concatenate([weight, spare], axis=0).T[:, :stored]
    columns = [turned_weight * scale_ref[j : j + 1, :] / math.sqrt(TERMS) for j in range(doc_blocks)]
    for block in range(stored):
        span = slice(block * width, (block + 1) * width)
        prior = prior_ref[span, :].astype(jnp.float32)
        for j in range(doc_blocks):
            basis[j, span, :] = (prior * columns[j][:, block : block + 1]).astype(jnp.bfloat16)
    for j in range(doc_blocks):
        partial_ref[j * docs : (j + 1) * docs, :] = jnp.dot(
            turned_ref[j * docs : (j + 1) * docs, :], basis[j], preferred_element_type=jnp.float32
        )


def project(core, keep, come, scales, prior, turned, total_docs):
    height, rank_size = prior.shape
    docs = turned.shape[0]
    doc_blocks = scales.shape[1]
    vmem = pl.BlockSpec(memory_space=pltpu.VMEM)
    return pl.pallas_call(
        functools.partial(project_kernel, total_docs),
        in_specs=[pl.BlockSpec(memory_space=pltpu.SMEM)] + [vmem] * 5,
        out_specs=vmem,
        out_shape=jax.ShapeDtypeStruct((docs, rank_size), jnp.float32),
        scratch_shapes=[pltpu.VMEM((doc_blocks, height, rank_size), jnp.bfloat16)],
        compiler_params=pltpu.CompilerParams(vmem_limit_bytes=32 * 2**20),
    )(core.reshape(1).astype(jnp.int32), keep, come, scales.T, prior, turned)


def shards(tf_blocks, block_scale, term_blocks, prior_rows, prior_sv):
    counts = tf_blocks[0]
    scales = block_scale[0]
    block_ids = term_blocks[0]
    basis_rows = prior_rows[0]
    stored_blocks = block_ids.shape[0]
    batch_docs = counts.shape[1]
    rank_size = basis_rows.shape[1]
    planes, lines = lax.axis_size("z"), lax.axis_size("y")
    doc_count = planes * lines * lax.axis_size("core")
    term_count = lax.axis_size("term")
    total_docs = batch_docs * doc_count
    share_docs = batch_docs // term_count
    pieces = mass_pieces(counts, scales, block_ids, doc_count)
    incoming = all_to_all(pieces.reshape(doc_count, 1, -1), ("z", "y", "core"))
    turned = counts.T
    chip = lax.axis_index("z") * lines + lax.axis_index("y")
    core = lax.axis_index("core")
    keep, send = find_masses(incoming.reshape(-1, LANES), chip, core, stored_blocks)
    come = swap_cores(send)
    partial = project(core, keep, come, scales, basis_rows, turned, total_docs)
    partial = partial.reshape(term_count, share_docs, rank_size)
    share_rows = jnp.sum(all_to_all(partial, "term"), axis=0)
    own_gram = jnp.dot(share_rows.T, share_rows, precision=highest) / total_docs
    flat_gram = jnp.concatenate([own_gram[:, t : t + LANES] for t in range(0, rank_size, LANES)])
    plane = ("y", "term")
    across = ("z", "core")
    plane_count = lines * term_count
    plane_gram = jnp.sum(all_to_all(flat_gram.reshape(plane_count, -1, LANES), plane), axis=0)
    piece_gram = jnp.sum(all_to_all(repeat(plane_gram, doc_count // lines), across), axis=0)
    flat_gram = all_to_all(repeat(piece_gram, plane_count), plane).reshape(-1, LANES)
    window = jnp.concatenate(
        [flat_gram[t : t + rank_size] for t in range(0, flat_gram.shape[0], rank_size)], axis=1
    )
    doc_coords, new_rows, singular = finish(window, prior_sv, share_rows, basis_rows)
    return (doc_coords, new_rows[None], singular.reshape(rank_size))


def solution(mesh):
    planes = lines = 8
    named = Mesh(
        mesh.devices.reshape(planes, lines, -1, mesh.shape["term"]), ("z", "y", "core", "term")
    )
    doc = ("z", "y", "core")
    in_specs = (
        P(doc, "term", None),
        P(doc, "term", None),
        P(doc, "term"),
        P(doc, "term", None),
        P(),
    )
    out_specs = (P(doc + ("term",), None), P(doc, "term", None), P())
    return jax.shard_map(shards, mesh=named, in_specs=in_specs, out_specs=out_specs, check_vma=False)
```

```python
import functools
import math

import jax
import jax.numpy as jnp
from jax import lax
from jax.experimental import pallas as pl
from jax.experimental.pallas import tpu as pltpu
from jax.sharding import Mesh
from jax.sharding import PartitionSpec as P

TERMS = 131072
ITERS = 4
LANES = 128
PANEL = 16
OUTER = 128


forget_factor = 0.85
highest = lax.Precision.HIGHEST


def contract(a, b, a_dim, b_dim):
    return lax.dot_general(
        a,
        b,
        (((a_dim,), (b_dim,)), ((), ())),
        precision=highest,
        preferred_element_type=jnp.float32,
    )


def eliminate(panel, first):
    size = panel.shape[0]
    rows = lax.broadcasted_iota(jnp.int32, (size, LANES), 0)
    columns = [
        jnp.broadcast_to(panel[:, first + k : first + k + 1], (size, LANES)) for k in range(size)
    ]
    tiles = [panel[:, t : t + LANES] for t in range(0, panel.shape[1], LANES)]
    pivots = jnp.zeros((size, LANES), jnp.float32)
    for k in range(size):
        pivot = columns[k][k : k + 1, :]
        pivots = jnp.where(rows == k, jnp.broadcast_to(pivot, (size, LANES)), pivots)
        if k + 1 < size:
            factor = jnp.where(rows > k, columns[k] * (1.0 / pivot), 0.0)
            for m in range(k + 1, size):
                columns[m] = columns[m] - factor * columns[m][k : k + 1, :]
            tiles = [tile - factor * tile[k : k + 1, :] for tile in tiles]
    root = lax.rsqrt(pivots)
    return jnp.concatenate([tile * root for tile in tiles], axis=1)


def split(value):
    high = value.astype(jnp.bfloat16)
    rest = value - high.astype(jnp.float32)
    middle = rest.astype(jnp.bfloat16)
    return high, middle, (rest - middle.astype(jnp.float32)).astype(jnp.bfloat16)


def fold(rows, second):
    high, middle, low = split(rows)
    right = jnp.concatenate([high, middle, high, middle, low, high], axis=0)
    left = jnp.concatenate([high, high, middle, middle, high, low], axis=0)
    return lax.dot_general(
        left[:, second : second + PANEL],
        right,
        (((0,), (0,)), ((), ())),
        preferred_element_type=jnp.float32,
    )


def orthonormal_rows(work):
    size = work.shape[0]
    for outer in range(0, size, OUTER):
        end = min(outer + OUTER, size)
        panel = work[outer : outer + PANEL, :]
        for first in range(outer, end, PANEL):
            second = first + PANEL
            if second < end:
                ahead = work[second : second + PANEL, :]
                if first > outer:
                    ahead = ahead - contract(work[outer:first, second : second + PANEL], work[outer:first, :], 0, 0)
            rows = eliminate(panel, first)
            work[first:second, :] = rows
            if second < end:
                panel = ahead - fold(rows, second)
        if end < size:
            work[end:, :] = work[end:, :] - contract(work[outer:end, end:size], work[outer:end, :], 0, 0)


def normalise(work):
    size = work.shape[0]
    image = work[:, size:]
    work[:, :size] = contract(image, image, 1, 1)
    orthonormal_rows(work)


def rotate(
    window_ref, sv_ref, share_ref, prior_hbm,
    coords_ref, rows_hbm, singular_ref,
    gram, work, rotation, prior, rows, load, store,
):
    loading = pltpu.make_async_copy(prior_hbm, prior, load)
    loading.start()
    size = window_ref.shape[0]
    row = lax.broadcasted_iota(jnp.int32, (size, size), 0)
    column = lax.broadcasted_iota(jnp.int32, (size, size), 1)
    sv = sv_ref[...]
    whole = window_ref[...] + jnp.where(row == column, forget_factor * sv * sv, 0.0)
    gram[...] = whole
    diagonal = jnp.where(row == column, whole, 0.0)
    top = jnp.max(jnp.max(diagonal, axis=0, keepdims=True), axis=1, keepdims=True)
    scaled = whole * (1.0 / top)
    square = contract(scaled, scaled, 1, 0)
    work[:, size:] = contract(square, square, 1, 0)
    normalise(work)
    result = work[:, size:]
    miss = contract(result, result, 1, 1) - jnp.where(row == column, 1.0, 0.0)
    half = jnp.where(row > column, miss, jnp.where(row == column, 0.5 * miss, 0.0))
    rotation[...] = result - contract(half, result, 1, 0)
    sound = jnp.sum(miss * miss) < 1e-2

    @pl.when(jnp.logical_not(sound))
    def _():
        work[:, size:] = gram[...]

        def step(iteration, carry):
            normalise(work)
            rotation[...] = work[:, size:]
            work[:, size:] = contract(rotation[...], gram[...], 1, 0)
            return carry

        lax.fori_loop(0, ITERS, step, 0)

    turned = rotation[...]
    turned_half = turned.astype(jnp.bfloat16)
    loading.wait()
    parts = store.shape[0]
    height = rows.shape[0] // parts
    storing = []
    for part in range(parts):
        span = pl.ds(part * height, height)
        rows[span, :] = lax.dot_general(
            prior[span, :], turned_half, (((1,), (1,)), ((), ())), preferred_element_type=jnp.float32
        ).astype(jnp.bfloat16)
        copy = pltpu.make_async_copy(rows.at[span], rows_hbm.at[span], store.at[part])
        copy.start()
        storing.append(copy)
    coords_ref[...] = contract(share_ref[...], turned, 1, 1)
    energy = turned * contract(turned, gram[...], 1, 0)
    total = contract(jnp.ones((8, size), jnp.float32), energy, 1, 1)
    singular_ref[...] = jnp.sqrt(total[:1])
    for copy in storing:
        copy.wait()


def all_to_all(pieces, axes):
    return lax.all_to_all(pieces, axes, 0, 0, tiled=True)


def repeat(piece, count):
    return jnp.broadcast_to(piece[None], (count,) + piece.shape)


def swap_cores(array):
    return lax.ppermute(array, "core", [(0, 1), (1, 0)])


def finish(window, prior_sv, share_rows, basis_rows):
    height, rank_size = basis_rows.shape
    parts = 4
    return pl.pallas_call(
        rotate,
        in_specs=[pl.BlockSpec(memory_space=pltpu.VMEM)] * 3 + [pl.BlockSpec(memory_space=pl.ANY)],
        out_specs=(
            pl.BlockSpec(memory_space=pltpu.VMEM),
            pl.BlockSpec(memory_space=pl.ANY),
            pl.BlockSpec(memory_space=pltpu.VMEM),
        ),
        out_shape=(
            jax.ShapeDtypeStruct(share_rows.shape, jnp.float32),
            jax.ShapeDtypeStruct((height, rank_size), jnp.bfloat16),
            jax.ShapeDtypeStruct((1, rank_size), jnp.float32),
        ),
        scratch_shapes=[
            pltpu.VMEM((rank_size, rank_size), jnp.float32),
            pltpu.VMEM((rank_size, 2 * rank_size), jnp.float32),
            pltpu.VMEM((rank_size, rank_size), jnp.float32),
            pltpu.VMEM((height, rank_size), jnp.bfloat16),
            pltpu.VMEM((height, rank_size), jnp.bfloat16),
            pltpu.SemaphoreType.DMA,
            pltpu.SemaphoreType.DMA((parts,)),
        ],
        compiler_params=pltpu.CompilerParams(vmem_limit_bytes=32 * 2**20),
    )(window, prior_sv.reshape(1, rank_size), share_rows, basis_rows)


def mass_pieces_kernel(slots, counts_ref, scale_ref, ids_ref, pieces_ref, mass):
    step = pl.program_id(0)
    width = counts_ref.shape[0] // slots
    docs = counts_ref.shape[1]
    doc_blocks = scale_ref.shape[0]
    marker = (
        lax.broadcasted_iota(jnp.int32, (16, docs), 1) // (docs // doc_blocks)
        == lax.broadcasted_iota(jnp.int32, (16, docs), 0)
    ).astype(jnp.bfloat16)
    for slot in range(slots):
        block = counts_ref[slot * width : (slot + 1) * width, :]
        sums = lax.dot_general(
            marker, block, (((1,), (1,)), ((), ())), preferred_element_type=jnp.float32
        )
        place = step * slots + slot
        total = sums[0:1] * scale_ref[0, place]
        for j in range(1, doc_blocks):
            total = total + sums[j : j + 1] * scale_ref[j, place]
        mass[pl.ds(place, 1), :] = total

    @pl.when(step == pl.num_programs(0) - 1)
    def _():
        stored = mass.shape[0]
        even = jnp.concatenate([mass[q : q + 1, :] for q in range(0, stored, 2)], axis=0)
        odd = jnp.concatenate([mass[q : q + 1, :] for q in range(1, stored, 2)], axis=0)
        half = LANES // 2
        lower = lax.broadcasted_iota(jnp.int32, even.shape, 1) < half
        near = jnp.where(lower, even, pltpu.roll(odd, half, 1))
        far = jnp.where(lower, pltpu.roll(even, half, 1), odd)
        ids = jnp.concatenate(
            [ids_ref[...].astype(jnp.float32), jnp.full((1, LANES - stored), -1.0, jnp.float32)], axis=1
        )
        period = jnp.concatenate([near, ids, far, ids] * 4, axis=0)
        rows = period.shape[0]
        for part in range(pieces_ref.shape[0] // rows):
            pieces_ref[part * rows : (part + 1) * rows, :] = period


def mass_pieces(counts, scales, block_ids, doc_count):
    height, docs = counts.shape
    stored = block_ids.shape[0]
    steps = 2
    return pl.pallas_call(
        functools.partial(mass_pieces_kernel, stored // steps),
        grid=(steps,),
        in_specs=[
            pl.BlockSpec((height // steps, docs), lambda i: (i, 0)),
            pl.BlockSpec(memory_space=pltpu.SMEM),
            pl.BlockSpec((1, stored), lambda i: (0, 0)),
        ],
        out_specs=pl.BlockSpec((doc_count * (stored // 2 + 1), LANES), lambda i: (0, 0)),
        out_shape=jax.ShapeDtypeStruct((doc_count * (stored // 2 + 1), LANES), jnp.float32),
        scratch_shapes=[pltpu.VMEM((stored, height // stored), jnp.float32)],
        compiler_params=pltpu.CompilerParams(vmem_limit_bytes=56 * 2**20),
    )(counts, scales.T, block_ids.reshape(1, stored))


def turn_kernel(after_ref, counts_ref, turned_ref):
    turned_ref[...] = counts_ref[...].T


def turn(counts, after):
    height, docs = counts.shape
    steps = 4
    return pl.pallas_call(
        turn_kernel,
        grid=(steps,),
        in_specs=[
            pl.BlockSpec(memory_space=pl.ANY),
            pl.BlockSpec((height // steps, docs), lambda i: (i, 0)),
        ],
        out_specs=pl.BlockSpec((docs, height // steps), lambda i: (0, i)),
        out_shape=jax.ShapeDtypeStruct((docs, height), counts.dtype),
        compiler_params=pltpu.CompilerParams(vmem_limit_bytes=16 * 2**20),
        cost_estimate=pl.CostEstimate(
            flops=0, bytes_accessed=4 * height * docs, transcendentals=0
        ),
    )(after, counts)


def find_masses_kernel(stored, place_ref, incoming_ref, before_ref, keep_ref, send_ref):
    piece = stored // 2 + 1
    batches = incoming_ref.shape[0] // piece
    half = LANES // 2
    chip, core = place_ref[0], place_ref[1]
    ids = incoming_ref[pl.ds(piece - 1, batches, stride=piece), :].T[:stored]
    batch = lax.broadcasted_iota(jnp.int32, ids.shape, 1)
    pair = [
        jnp.sum(jnp.where(batch == 2 * chip + side, ids, 0.0), axis=1, keepdims=True)
        for side in (0, 1)
    ]
    wanted = jnp.broadcast_to(jnp.concatenate(pair, axis=0), (2 * stored, batches))
    matches, parts = [], [[], [], []]
    for row in range(piece - 1):
        masses = incoming_ref[pl.ds(row, batches, stride=piece), :]
        high = masses.astype(jnp.bfloat16)
        rest = masses - high.astype(jnp.float32)
        low = rest.astype(jnp.bfloat16)
        last = (rest - low.astype(jnp.float32)).astype(jnp.bfloat16)
        for part, value in zip(parts, (high, low, last)):
            part.append(value)
        match = [
            jnp.where(wanted == ids[2 * row + slot : 2 * row + slot + 1], 1.0, 0.0)
            for slot in range(2)
        ]
        matches.append(jnp.concatenate(match, axis=0).astype(jnp.bfloat16))
    matches = jnp.concatenate(matches, axis=1)
    found = 0.0
    for part in parts:
        found = found + jnp.dot(
            matches, jnp.concatenate(part, axis=0), preferred_element_type=jnp.float32
        )
    masses = found[: 2 * stored, :half] + found[2 * stored :, half:]
    mine = core == 0
    keep_ref[...] = jnp.where(mine, masses[:stored], masses[stored:])
    send_ref[...] = jnp.where(mine, masses[stored:], masses[:stored])


def find_masses(incoming, before, chip, core, stored):
    shape = jax.ShapeDtypeStruct((stored, LANES // 2), jnp.float32)
    return pl.pallas_call(
        functools.partial(find_masses_kernel, stored),
        in_specs=[
            pl.BlockSpec(memory_space=pltpu.SMEM),
            pl.BlockSpec(memory_space=pltpu.VMEM),
            pl.BlockSpec(memory_space=pl.ANY),
        ],
        out_specs=(pl.BlockSpec(memory_space=pltpu.VMEM), pl.BlockSpec(memory_space=pltpu.VMEM)),
        out_shape=(shape, shape),
        compiler_params=pltpu.CompilerParams(vmem_limit_bytes=16 * 2**20),
    )(jnp.stack([chip, core]).astype(jnp.int32), incoming, before)


def project_kernel(
    total_docs, core_ref, keep_ref, come_ref, scale_ref, prior_ref, turned_ref, partial_ref, basis
):
    stored = keep_ref.shape[0]
    doc_blocks = scale_ref.shape[0]
    height = prior_ref.shape[0]
    width = height // stored
    docs = partial_ref.shape[0] // doc_blocks
    mine, other = keep_ref[...], come_ref[...]
    first = core_ref[0] == 0
    term_mass = jnp.concatenate(
        [jnp.where(first, mine, other), jnp.where(first, other, mine)], axis=1
    )
    weight = jnp.log(1.0 + total_docs / (1.0 + term_mass))
    spare = jnp.zeros((LANES - stored, LANES), jnp.float32)
    turned_weight = jnp.concatenate([weight, spare], axis=0).T[:, :stored]
    columns = [turned_weight * scale_ref[j : j + 1, :] / math.sqrt(TERMS) for j in range(doc_blocks)]
    for block in range(stored):
        span = slice(block * width, (block + 1) * width)
        prior = prior_ref[span, :].astype(jnp.float32)
        for j in range(doc_blocks):
            basis[j, span, :] = (prior * columns[j][:, block : block + 1]).astype(jnp.bfloat16)
    for j in range(doc_blocks):
        partial_ref[j * docs : (j + 1) * docs, :] = jnp.dot(
            turned_ref[j * docs : (j + 1) * docs, :], basis[j], preferred_element_type=jnp.float32
        )


def project(core, keep, come, scales, prior, turned, total_docs):
    height, rank_size = prior.shape
    docs = turned.shape[0]
    doc_blocks = scales.shape[1]
    vmem = pl.BlockSpec(memory_space=pltpu.VMEM)
    return pl.pallas_call(
        functools.partial(project_kernel, total_docs),
        in_specs=[pl.BlockSpec(memory_space=pltpu.SMEM)] + [vmem] * 5,
        out_specs=vmem,
        out_shape=jax.ShapeDtypeStruct((docs, rank_size), jnp.float32),
        scratch_shapes=[pltpu.VMEM((doc_blocks, height, rank_size), jnp.bfloat16)],
        compiler_params=pltpu.CompilerParams(vmem_limit_bytes=32 * 2**20),
    )(core.reshape(1).astype(jnp.int32), keep, come, scales.T, prior, turned)


def shards(tf_blocks, block_scale, term_blocks, prior_rows, prior_sv):
    counts = tf_blocks[0]
    scales = block_scale[0]
    block_ids = term_blocks[0]
    basis_rows = prior_rows[0]
    stored_blocks = block_ids.shape[0]
    batch_docs = counts.shape[1]
    rank_size = basis_rows.shape[1]
    planes, lines = lax.axis_size("z"), lax.axis_size("y")
    doc_count = planes * lines * lax.axis_size("core")
    term_count = lax.axis_size("term")
    total_docs = batch_docs * doc_count
    share_docs = batch_docs // term_count
    pieces = mass_pieces(counts, scales, block_ids, doc_count)
    incoming = all_to_all(pieces.reshape(doc_count, 1, -1), ("z", "y", "core"))
    turned = turn(counts, pieces[:8])
    chip = lax.axis_index("z") * lines + lax.axis_index("y")
    core = lax.axis_index("core")
    keep, send = find_masses(incoming.reshape(-1, LANES), turned, chip, core, stored_blocks)
    come = swap_cores(send)
    partial = project(core, keep, come, scales, basis_rows, turned, total_docs)
    partial = partial.reshape(term_count, share_docs, rank_size)
    share_rows = jnp.sum(all_to_all(partial, "term"), axis=0)
    own_gram = jnp.dot(share_rows.T, share_rows, precision=highest) / total_docs
    flat_gram = jnp.concatenate([own_gram[:, t : t + LANES] for t in range(0, rank_size, LANES)])
    plane = ("y", "term")
    across = ("z", "core")
    plane_count = lines * term_count
    plane_gram = jnp.sum(all_to_all(flat_gram.reshape(plane_count, -1, LANES), plane), axis=0)
    piece_gram = jnp.sum(all_to_all(repeat(plane_gram, doc_count // lines), across), axis=0)
    flat_gram = all_to_all(repeat(piece_gram, plane_count), plane).reshape(-1, LANES)
    window = jnp.concatenate(
        [flat_gram[t : t + rank_size] for t in range(0, flat_gram.shape[0], rank_size)], axis=1
    )
    doc_coords, new_rows, singular = finish(window, prior_sv, share_rows, basis_rows)
    return (doc_coords, new_rows[None], singular.reshape(rank_size))


def solution(mesh):
    planes = lines = 8
    named = Mesh(
        mesh.devices.reshape(planes, lines, -1, mesh.shape["term"]), ("z", "y", "core", "term")
    )
    doc = ("z", "y", "core")
    in_specs = (
        P(doc, "term", None),
        P(doc, "term", None),
        P(doc, "term"),
        P(doc, "term", None),
        P(),
    )
    out_specs = (P(doc + ("term",), None), P(doc, "term", None), P())
    return jax.shard_map(shards, mesh=named, in_specs=in_specs, out_specs=out_specs, check_vma=False)
```

```python
import functools
import math

import jax
import jax.numpy as jnp
from jax import lax
from jax.experimental import pallas as pl
from jax.experimental.pallas import tpu as pltpu
from jax.sharding import Mesh
from jax.sharding import PartitionSpec as P

TERMS = 131072
ITERS = 4
LANES = 128
PANEL = 32
HALF = 16
OUTER = 256


forget_factor = 0.85
highest = lax.Precision.HIGHEST


def contract(a, b, a_dim, b_dim):
    return lax.dot_general(
        a,
        b,
        (((a_dim,), (b_dim,)), ((), ())),
        precision=highest,
        preferred_element_type=jnp.float32,
    )


def eliminate(panel, first):
    height = panel.shape[0]
    rows = lax.broadcasted_iota(jnp.int32, (HALF, LANES), 0)
    parts = [
        [panel[top : top + HALF, t : t + LANES] for t in range(0, panel.shape[1], LANES)]
        for top in range(0, height, HALF)
    ]
    done = []
    while parts:
        lead, *below = parts
        start = first + len(done) * HALF
        tile, lane = start // LANES, start % LANES
        columns = [
            [jnp.broadcast_to(part[tile][:, lane + k : lane + k + 1], (HALF, LANES)) for k in range(HALF)]
            for part in parts
        ]
        pivots = jnp.zeros((HALF, LANES), jnp.float32)
        for k in range(HALF):
            pivot = columns[0][k][k : k + 1, :]
            pivots = jnp.where(rows == k, jnp.broadcast_to(pivot, (HALF, LANES)), pivots)
            unit = 1.0 / pivot
            factors = [jnp.where(rows > k, columns[0][k] * unit, 0.0)]
            factors += [column[k] * unit for column in columns[1:]]
            for m in range(k + 1, HALF):
                value = columns[0][m][k : k + 1, :]
                for column, factor in zip(columns, factors):
                    column[m] = column[m] - factor * value
            values = [entry[k : k + 1, :] for entry in lead]
            lead = [entry - factors[0] * value for entry, value in zip(lead, values)]
            below = [
                [entry - factor * value for entry, value in zip(part, values)]
                for part, factor in zip(below, factors[1:])
            ]
        root = lax.rsqrt(pivots)
        done.append(jnp.concatenate([entry * root for entry in lead], axis=1))
        parts = below
    return jnp.concatenate(done, axis=0)


def split(value):
    high = value.astype(jnp.bfloat16)
    rest = value - high.astype(jnp.float32)
    middle = rest.astype(jnp.bfloat16)
    return high, middle, (rest - middle.astype(jnp.float32)).astype(jnp.bfloat16)


def fold(rows, second):
    high, middle, low = split(rows)
    right = jnp.concatenate([high, middle, high, middle, low, high], axis=0)
    left = jnp.concatenate([high, high, middle, middle, high, low], axis=0)
    return lax.dot_general(
        left[:, second : second + PANEL],
        right,
        (((0,), (0,)), ((), ())),
        preferred_element_type=jnp.float32,
    )


def orthonormal_rows(work):
    size = work.shape[0]
    for outer in range(0, size, OUTER):
        end = min(outer + OUTER, size)
        panel = work[outer : outer + PANEL, :]
        for first in range(outer, end, PANEL):
            second = first + PANEL
            if second < end:
                ahead = work[second : second + PANEL, :]
                if first > outer:
                    ahead = ahead - contract(work[outer:first, second : second + PANEL], work[outer:first, :], 0, 0)
            rows = eliminate(panel, first)
            work[first:second, :] = rows
            if second < end:
                panel = ahead - fold(rows, second)
        if end < size:
            work[end:, :] = work[end:, :] - contract(work[outer:end, end:size], work[outer:end, :], 0, 0)


def normalise(work):
    size = work.shape[0]
    image = work[:, size:]
    work[:, :size] = contract(image, image, 1, 1)
    orthonormal_rows(work)


def pack(matrix):
    half = LANES // 2
    lower = lax.broadcasted_iota(jnp.int32, (half, LANES), 1) < half
    inner = pltpu.roll(matrix[half:LANES, :LANES], half, 1)
    corner = matrix[LANES + half :, LANES:]
    return jnp.concatenate(
        [
            matrix[:half, :LANES],
            matrix[:half, LANES:],
            matrix[half:LANES, LANES:],
            matrix[LANES : LANES + half, LANES:],
            jnp.where(lower, inner, corner),
        ],
        axis=0,
    )


def unpack(packed):
    half = LANES // 2
    blocks = [packed[top : top + half] for top in range(0, packed.shape[0], half)]
    spare = jnp.zeros((half, LANES), jnp.float32)
    left = jnp.concatenate([blocks[0], pltpu.roll(blocks[4], half, 1), spare, spare], axis=0)
    right = jnp.concatenate([blocks[1], blocks[2], blocks[3], blocks[4]], axis=0)
    upper = jnp.concatenate([left, right], axis=1)
    row = lax.broadcasted_iota(jnp.int32, upper.shape, 0) // half
    column = lax.broadcasted_iota(jnp.int32, upper.shape, 1) // half
    return jnp.where(row <= column, upper, upper.T)


def own_gram_kernel(total_docs, incoming_ref, share_ref, packed_ref):
    share = jnp.sum(incoming_ref[...], axis=0)
    share_ref[...] = share
    packed_ref[...] = pack(contract(share, share, 0, 0) * (1.0 / total_docs))


def own_gram(incoming, total_docs):
    docs, rank_size = incoming.shape[1:]
    vmem = pl.BlockSpec(memory_space=pltpu.VMEM)
    return pl.pallas_call(
        functools.partial(own_gram_kernel, total_docs),
        in_specs=[vmem],
        out_specs=(vmem, vmem),
        out_shape=(
            jax.ShapeDtypeStruct((docs, rank_size), jnp.float32),
            jax.ShapeDtypeStruct((5 * LANES // 2, LANES), jnp.float32),
        ),
        compiler_params=pltpu.CompilerParams(vmem_limit_bytes=8 * 2**20),
    )(incoming)


def rotate(
    packed_ref, sv_ref, share_ref, prior_hbm,
    coords_ref, rows_hbm, singular_ref,
    gram, work, rotation, prior, rows, load, store,
):
    loading = pltpu.make_async_copy(prior_hbm, prior, load)
    loading.start()
    size = sv_ref.shape[1]
    row = lax.broadcasted_iota(jnp.int32, (size, size), 0)
    column = lax.broadcasted_iota(jnp.int32, (size, size), 1)
    sv = sv_ref[...]
    whole = unpack(packed_ref[...]) + jnp.where(row == column, forget_factor * sv * sv, 0.0)
    gram[...] = whole
    diagonal = jnp.where(row == column, whole, 0.0)
    top = jnp.max(jnp.max(diagonal, axis=0, keepdims=True), axis=1, keepdims=True)
    scaled = whole * (1.0 / top)
    square = contract(scaled, scaled, 1, 0)
    work[:, size:] = contract(square, square, 1, 0)
    normalise(work)
    result = work[:, size:]
    miss = contract(result, result, 1, 1) - jnp.where(row == column, 1.0, 0.0)
    half = jnp.where(row > column, miss, jnp.where(row == column, 0.5 * miss, 0.0))
    rotation[...] = result - contract(half, result, 1, 0)
    sound = jnp.sum(miss * miss) < 1e-2

    @pl.when(jnp.logical_not(sound))
    def _():
        work[:, size:] = gram[...]

        def step(iteration, carry):
            normalise(work)
            rotation[...] = work[:, size:]
            work[:, size:] = contract(rotation[...], gram[...], 1, 0)
            return carry

        lax.fori_loop(0, ITERS, step, 0)

    turned = rotation[...]
    turned_half = turned.astype(jnp.bfloat16)
    loading.wait()
    parts = store.shape[0]
    height = rows.shape[0] // parts
    storing = []
    for part in range(parts):
        span = pl.ds(part * height, height)
        rows[span, :] = lax.dot_general(
            prior[span, :], turned_half, (((1,), (1,)), ((), ())), preferred_element_type=jnp.float32
        ).astype(jnp.bfloat16)
        copy = pltpu.make_async_copy(rows.at[span], rows_hbm.at[span], store.at[part])
        copy.start()
        storing.append(copy)
    coords_ref[...] = contract(share_ref[...], turned, 1, 1)
    energy = turned * contract(turned, gram[...], 1, 0)
    total = contract(jnp.ones((8, size), jnp.float32), energy, 1, 1)
    singular_ref[...] = jnp.sqrt(total[:1])
    for copy in storing:
        copy.wait()


def all_to_all(pieces, axes):
    return lax.all_to_all(pieces, axes, 0, 0, tiled=True)


def repeat(piece, count):
    return jnp.broadcast_to(piece[None], (count,) + piece.shape)


def swap_cores(array):
    return lax.ppermute(array, "core", [(0, 1), (1, 0)])


def finish(packed, prior_sv, share_rows, basis_rows):
    height, rank_size = basis_rows.shape
    parts = 4
    return pl.pallas_call(
        rotate,
        in_specs=[pl.BlockSpec(memory_space=pltpu.VMEM)] * 3 + [pl.BlockSpec(memory_space=pl.ANY)],
        out_specs=(
            pl.BlockSpec(memory_space=pltpu.VMEM),
            pl.BlockSpec(memory_space=pl.ANY),
            pl.BlockSpec(memory_space=pltpu.VMEM),
        ),
        out_shape=(
            jax.ShapeDtypeStruct(share_rows.shape, jnp.float32),
            jax.ShapeDtypeStruct((height, rank_size), jnp.bfloat16),
            jax.ShapeDtypeStruct((1, rank_size), jnp.float32),
        ),
        scratch_shapes=[
            pltpu.VMEM((rank_size, rank_size), jnp.float32),
            pltpu.VMEM((rank_size, 2 * rank_size), jnp.float32),
            pltpu.VMEM((rank_size, rank_size), jnp.float32),
            pltpu.VMEM((height, rank_size), jnp.bfloat16),
            pltpu.VMEM((height, rank_size), jnp.bfloat16),
            pltpu.SemaphoreType.DMA,
            pltpu.SemaphoreType.DMA((parts,)),
        ],
        compiler_params=pltpu.CompilerParams(vmem_limit_bytes=32 * 2**20),
    )(packed, prior_sv.reshape(1, rank_size), share_rows, basis_rows)


def mass_pieces_kernel(slots, counts_ref, scale_ref, ids_ref, pieces_ref, mass):
    step = pl.program_id(0)
    width = counts_ref.shape[0] // slots
    docs = counts_ref.shape[1]
    doc_blocks = scale_ref.shape[0]
    marker = (
        lax.broadcasted_iota(jnp.int32, (16, docs), 1) // (docs // doc_blocks)
        == lax.broadcasted_iota(jnp.int32, (16, docs), 0)
    ).astype(jnp.bfloat16)
    for slot in range(slots):
        block = counts_ref[slot * width : (slot + 1) * width, :]
        sums = lax.dot_general(
            marker, block, (((1,), (1,)), ((), ())), preferred_element_type=jnp.float32
        )
        place = step * slots + slot
        total = sums[0:1] * scale_ref[0, place]
        for j in range(1, doc_blocks):
            total = total + sums[j : j + 1] * scale_ref[j, place]
        mass[pl.ds(place, 1), :] = total

    @pl.when(step == pl.num_programs(0) - 1)
    def _():
        stored = mass.shape[0]
        even = jnp.concatenate([mass[q : q + 1, :] for q in range(0, stored, 2)], axis=0)
        odd = jnp.concatenate([mass[q : q + 1, :] for q in range(1, stored, 2)], axis=0)
        half = LANES // 2
        lower = lax.broadcasted_iota(jnp.int32, even.shape, 1) < half
        near = jnp.where(lower, even, pltpu.roll(odd, half, 1))
        far = jnp.where(lower, pltpu.roll(even, half, 1), odd)
        ids = jnp.concatenate(
            [ids_ref[...].astype(jnp.float32), jnp.full((1, LANES - stored), -1.0, jnp.float32)], axis=1
        )
        period = jnp.concatenate([near, ids, far, ids] * 4, axis=0)
        rows = period.shape[0]
        for part in range(pieces_ref.shape[0] // rows):
            pieces_ref[part * rows : (part + 1) * rows, :] = period


def mass_pieces(counts, scales, block_ids, doc_count):
    height, docs = counts.shape
    stored = block_ids.shape[0]
    steps = 2
    return pl.pallas_call(
        functools.partial(mass_pieces_kernel, stored // steps),
        grid=(steps,),
        in_specs=[
            pl.BlockSpec((height // steps, docs), lambda i: (i, 0)),
            pl.BlockSpec(memory_space=pltpu.SMEM),
            pl.BlockSpec((1, stored), lambda i: (0, 0)),
        ],
        out_specs=pl.BlockSpec((doc_count * (stored // 2 + 1), LANES), lambda i: (0, 0)),
        out_shape=jax.ShapeDtypeStruct((doc_count * (stored // 2 + 1), LANES), jnp.float32),
        scratch_shapes=[pltpu.VMEM((stored, height // stored), jnp.float32)],
        compiler_params=pltpu.CompilerParams(vmem_limit_bytes=56 * 2**20),
    )(counts, scales.T, block_ids.reshape(1, stored))


def turn_kernel(after_ref, counts_ref, turned_ref):
    turned_ref[...] = counts_ref[...].T


def turn(counts, after):
    height, docs = counts.shape
    steps = 4
    return pl.pallas_call(
        turn_kernel,
        grid=(steps,),
        in_specs=[
            pl.BlockSpec(memory_space=pl.ANY),
            pl.BlockSpec((height // steps, docs), lambda i: (i, 0)),
        ],
        out_specs=pl.BlockSpec((docs, height // steps), lambda i: (0, i)),
        out_shape=jax.ShapeDtypeStruct((docs, height), counts.dtype),
        compiler_params=pltpu.CompilerParams(vmem_limit_bytes=6 * 2**20),
        cost_estimate=pl.CostEstimate(
            flops=0, bytes_accessed=4 * height * docs, transcendentals=0
        ),
    )(after, counts)


def find_masses_kernel(stored, place_ref, incoming_ref, before_ref, keep_ref, send_ref):
    piece = stored // 2 + 1
    batches = incoming_ref.shape[0] // piece
    half = LANES // 2
    chip, core = place_ref[0], place_ref[1]
    ids = incoming_ref[pl.ds(piece - 1, batches, stride=piece), :].T[:stored]
    batch = lax.broadcasted_iota(jnp.int32, ids.shape, 1)
    pair = [
        jnp.sum(jnp.where(batch == 2 * chip + side, ids, 0.0), axis=1, keepdims=True)
        for side in (0, 1)
    ]
    wanted = jnp.broadcast_to(jnp.concatenate(pair, axis=0), (2 * stored, batches))
    matches, parts = [], [[], [], []]
    for row in range(piece - 1):
        masses = incoming_ref[pl.ds(row, batches, stride=piece), :]
        high = masses.astype(jnp.bfloat16)
        rest = masses - high.astype(jnp.float32)
        low = rest.astype(jnp.bfloat16)
        last = (rest - low.astype(jnp.float32)).astype(jnp.bfloat16)
        for part, value in zip(parts, (high, low, last)):
            part.append(value)
        match = [
            jnp.where(wanted == ids[2 * row + slot : 2 * row + slot + 1], 1.0, 0.0)
            for slot in range(2)
        ]
        matches.append(jnp.concatenate(match, axis=0).astype(jnp.bfloat16))
    matches = jnp.concatenate(matches, axis=1)
    found = 0.0
    for part in parts:
        found = found + jnp.dot(
            matches, jnp.concatenate(part, axis=0), preferred_element_type=jnp.float32
        )
    masses = found[: 2 * stored, :half] + found[2 * stored :, half:]
    mine = core == 0
    keep_ref[...] = jnp.where(mine, masses[:stored], masses[stored:])
    send_ref[...] = jnp.where(mine, masses[stored:], masses[:stored])


def find_masses(incoming, before, chip, core, stored):
    shape = jax.ShapeDtypeStruct((stored, LANES // 2), jnp.float32)
    return pl.pallas_call(
        functools.partial(find_masses_kernel, stored),
        in_specs=[
            pl.BlockSpec(memory_space=pltpu.SMEM),
            pl.BlockSpec(memory_space=pltpu.VMEM),
            pl.BlockSpec(memory_space=pl.ANY),
        ],
        out_specs=(pl.BlockSpec(memory_space=pltpu.VMEM), pl.BlockSpec(memory_space=pltpu.VMEM)),
        out_shape=(shape, shape),
        compiler_params=pltpu.CompilerParams(vmem_limit_bytes=6 * 2**20),
    )(jnp.stack([chip, core]).astype(jnp.int32), incoming, before)


def project_kernel(
    total_docs, core_ref, keep_ref, come_ref, scale_ref, prior_ref, turned_ref, partial_ref, basis
):
    stored = keep_ref.shape[0]
    doc_blocks = scale_ref.shape[0]
    height = prior_ref.shape[0]
    width = height // stored
    docs = partial_ref.shape[0] // doc_blocks
    mine, other = keep_ref[...], come_ref[...]
    first = core_ref[0] == 0
    term_mass = jnp.concatenate(
        [jnp.where(first, mine, other), jnp.where(first, other, mine)], axis=1
    )
    weight = jnp.log(1.0 + total_docs / (1.0 + term_mass))
    spare = jnp.zeros((LANES - stored, LANES), jnp.float32)
    turned_weight = jnp.concatenate([weight, spare], axis=0).T[:, :stored]
    columns = [turned_weight * scale_ref[j : j + 1, :] / math.sqrt(TERMS) for j in range(doc_blocks)]
    for block in range(stored):
        span = slice(block * width, (block + 1) * width)
        prior = prior_ref[span, :].astype(jnp.float32)
        for j in range(doc_blocks):
            basis[j, span, :] = (prior * columns[j][:, block : block + 1]).astype(jnp.bfloat16)
    for j in range(doc_blocks):
        partial_ref[j * docs : (j + 1) * docs, :] = jnp.dot(
            turned_ref[j * docs : (j + 1) * docs, :], basis[j], preferred_element_type=jnp.float32
        )


def project(core, keep, come, scales, prior, turned, total_docs):
    height, rank_size = prior.shape
    docs = turned.shape[0]
    doc_blocks = scales.shape[1]
    vmem = pl.BlockSpec(memory_space=pltpu.VMEM)
    return pl.pallas_call(
        functools.partial(project_kernel, total_docs),
        in_specs=[pl.BlockSpec(memory_space=pltpu.SMEM)] + [vmem] * 5,
        out_specs=vmem,
        out_shape=jax.ShapeDtypeStruct((docs, rank_size), jnp.float32),
        scratch_shapes=[pltpu.VMEM((doc_blocks, height, rank_size), jnp.bfloat16)],
        compiler_params=pltpu.CompilerParams(vmem_limit_bytes=32 * 2**20),
    )(core.reshape(1).astype(jnp.int32), keep, come, scales.T, prior, turned)


def shards(tf_blocks, block_scale, term_blocks, prior_rows, prior_sv):
    counts = tf_blocks[0]
    scales = block_scale[0]
    block_ids = term_blocks[0]
    basis_rows = prior_rows[0]
    stored_blocks = block_ids.shape[0]
    batch_docs = counts.shape[1]
    rank_size = basis_rows.shape[1]
    planes, lines = lax.axis_size("z"), lax.axis_size("y")
    doc_count = planes * lines * lax.axis_size("core")
    term_count = lax.axis_size("term")
    total_docs = batch_docs * doc_count
    share_docs = batch_docs // term_count
    pieces = mass_pieces(counts, scales, block_ids, doc_count)
    incoming = all_to_all(pieces.reshape(doc_count, 1, -1), ("z", "y", "core"))
    turned = turn(counts, pieces[:8])
    chip = lax.axis_index("z") * lines + lax.axis_index("y")
    core = lax.axis_index("core")
    keep, send = find_masses(incoming.reshape(-1, LANES), turned, chip, core, stored_blocks)
    come = swap_cores(send)
    partial = project(core, keep, come, scales, basis_rows, turned, total_docs)
    partial = partial.reshape(term_count, share_docs, rank_size)
    share_rows, packed = own_gram(all_to_all(partial, "term"), total_docs)
    plane = ("y", "term")
    across = ("z", "core")
    plane_count = lines * term_count
    plane_gram = jnp.sum(all_to_all(packed.reshape(plane_count, 1, -1), plane), axis=0)
    piece_gram = jnp.sum(all_to_all(repeat(plane_gram, doc_count // lines), across), axis=0)
    packed = all_to_all(repeat(piece_gram, plane_count), plane).reshape(-1, LANES)
    doc_coords, new_rows, singular = finish(packed, prior_sv, share_rows, basis_rows)
    return (doc_coords, new_rows[None], singular.reshape(rank_size))


def solution(mesh):
    planes = lines = 8
    named = Mesh(
        mesh.devices.reshape(planes, lines, -1, mesh.shape["term"]), ("z", "y", "core", "term")
    )
    doc = ("z", "y", "core")
    in_specs = (
        P(doc, "term", None),
        P(doc, "term", None),
        P(doc, "term"),
        P(doc, "term", None),
        P(),
    )
    out_specs = (P(doc + ("term",), None), P(doc, "term", None), P())
    return jax.shard_map(shards, mesh=named, in_specs=in_specs, out_specs=out_specs, check_vma=False)
```

```python
import functools
import math

import jax
import jax.numpy as jnp
from jax import lax
from jax.experimental import pallas as pl
from jax.experimental.pallas import tpu as pltpu
from jax.sharding import Mesh
from jax.sharding import PartitionSpec as P

TERMS = 131072
ITERS = 4
LANES = 128
PANEL = 32
HALF = 16


forget_factor = 0.85
highest = lax.Precision.HIGHEST


def contract(a, b, a_dim, b_dim):
    return lax.dot_general(
        a,
        b,
        (((a_dim,), (b_dim,)), ((), ())),
        precision=highest,
        preferred_element_type=jnp.float32,
    )


def eliminate(panel, first):
    height = panel.shape[0]
    rows = lax.broadcasted_iota(jnp.int32, (HALF, LANES), 0)
    parts = [
        [panel[top : top + HALF, t : t + LANES] for t in range(0, panel.shape[1], LANES)]
        for top in range(0, height, HALF)
    ]
    done = []
    while parts:
        lead, *below = parts
        start = first + len(done) * HALF
        tile, lane = start // LANES, start % LANES
        columns = [
            [jnp.broadcast_to(part[tile][:, lane + k : lane + k + 1], (HALF, LANES)) for k in range(HALF)]
            for part in parts
        ]
        pivots = jnp.zeros((HALF, LANES), jnp.float32)
        for k in range(HALF):
            pivot = columns[0][k][k : k + 1, :]
            pivots = jnp.where(rows == k, jnp.broadcast_to(pivot, (HALF, LANES)), pivots)
            unit = 1.0 / pivot
            factors = [jnp.where(rows > k, columns[0][k] * unit, 0.0)]
            factors += [column[k] * unit for column in columns[1:]]
            for m in range(k + 1, HALF):
                value = columns[0][m][k : k + 1, :]
                for column, factor in zip(columns, factors):
                    column[m] = column[m] - factor * value
            values = [entry[k : k + 1, :] for entry in lead]
            lead = [entry - factors[0] * value for entry, value in zip(lead, values)]
            below = [
                [entry - factor * value for entry, value in zip(part, values)]
                for part, factor in zip(below, factors[1:])
            ]
        root = lax.rsqrt(pivots)
        done.append(jnp.concatenate([entry * root for entry in lead], axis=1))
        parts = below
    return jnp.concatenate(done, axis=0)


def split(value):
    high = value.astype(jnp.bfloat16)
    rest = value - high.astype(jnp.float32)
    middle = rest.astype(jnp.bfloat16)
    return high, middle, (rest - middle.astype(jnp.float32)).astype(jnp.bfloat16)


def fold(rows, second):
    high, middle, low = split(rows)
    right = jnp.concatenate([high, middle, high, middle, low, high], axis=0)
    left = jnp.concatenate([high, high, middle, middle, high, low], axis=0)
    return lax.dot_general(
        left[:, second : second + PANEL],
        right,
        (((0,), (0,)), ((), ())),
        preferred_element_type=jnp.float32,
    )


def orthonormal_rows(work):
    size = work.shape[0]
    panel = work[:PANEL, :]
    for first in range(0, size, PANEL):
        second = first + PANEL
        left, later = first // LANES * LANES, second // LANES * LANES
        if second < size:
            ahead = work[second : second + PANEL, later:]
            if first > 0:
                ahead = ahead - contract(
                    work[:first, second : second + PANEL], work[:first, later:], 0, 0
                )
        rows = eliminate(panel, first - left)
        work[first:second, left:] = rows
        if second < size:
            panel = ahead - fold(rows[:, later - left :], second - later)


def normalise(work):
    size = work.shape[0]
    image = work[:, size:]
    work[:, :size] = contract(image, image, 1, 1)
    orthonormal_rows(work)


def pack(matrix):
    half = LANES // 2
    lower = lax.broadcasted_iota(jnp.int32, (half, LANES), 1) < half
    inner = pltpu.roll(matrix[half:LANES, :LANES], half, 1)
    corner = matrix[LANES + half :, LANES:]
    return jnp.concatenate(
        [
            matrix[:half, :LANES],
            matrix[:half, LANES:],
            matrix[half:LANES, LANES:],
            matrix[LANES : LANES + half, LANES:],
            jnp.where(lower, inner, corner),
        ],
        axis=0,
    )


def unpack(packed):
    half = LANES // 2
    blocks = [packed[top : top + half] for top in range(0, packed.shape[0], half)]
    spare = jnp.zeros((half, LANES), jnp.float32)
    left = jnp.concatenate([blocks[0], pltpu.roll(blocks[4], half, 1), spare, spare], axis=0)
    right = jnp.concatenate([blocks[1], blocks[2], blocks[3], blocks[4]], axis=0)
    upper = jnp.concatenate([left, right], axis=1)
    row = lax.broadcasted_iota(jnp.int32, upper.shape, 0) // half
    column = lax.broadcasted_iota(jnp.int32, upper.shape, 1) // half
    return jnp.where(row <= column, upper, upper.T)


def own_gram_kernel(total_docs, incoming_ref, share_ref, packed_ref):
    share = jnp.sum(incoming_ref[...], axis=0)
    share_ref[...] = share
    packed_ref[...] = pack(contract(share, share, 0, 0) * (1.0 / total_docs))


def own_gram(incoming, total_docs):
    docs, rank_size = incoming.shape[1:]
    vmem = pl.BlockSpec(memory_space=pltpu.VMEM)
    return pl.pallas_call(
        functools.partial(own_gram_kernel, total_docs),
        in_specs=[vmem],
        out_specs=(vmem, vmem),
        out_shape=(
            jax.ShapeDtypeStruct((docs, rank_size), jnp.float32),
            jax.ShapeDtypeStruct((5 * LANES // 2, LANES), jnp.float32),
        ),
        compiler_params=pltpu.CompilerParams(vmem_limit_bytes=8 * 2**20),
    )(incoming)


def near_contract(a, b, a_dim, b_dim):
    def halves(value):
        high = value.astype(jnp.bfloat16)
        return high, (value - high.astype(jnp.float32)).astype(jnp.bfloat16)

    (a_high, a_low), (b_high, b_low) = halves(a), halves(b)
    return lax.dot_general(
        jnp.concatenate([a_high, a_high, a_low], axis=a_dim),
        jnp.concatenate([b_high, b_low, b_high], axis=b_dim),
        (((a_dim,), (b_dim,)), ((), ())),
        preferred_element_type=jnp.float32,
    )


def rotate(
    packed_ref, sv_ref, share_ref, prior_hbm,
    coords_ref, rows_hbm, singular_ref,
    gram, work, rotation, prior, rows, load, store,
):
    loading = pltpu.make_async_copy(prior_hbm, prior, load)
    loading.start()
    size = sv_ref.shape[1]
    row = lax.broadcasted_iota(jnp.int32, (size, size), 0)
    column = lax.broadcasted_iota(jnp.int32, (size, size), 1)
    sv = sv_ref[...]
    whole = unpack(packed_ref[...]) + jnp.where(row == column, forget_factor * sv * sv, 0.0)
    gram[...] = whole
    diagonal = jnp.where(row == column, whole, 0.0)
    top = jnp.max(jnp.max(diagonal, axis=0, keepdims=True), axis=1, keepdims=True)
    scaled = whole * (1.0 / top)
    square = contract(scaled, scaled, 1, 0)
    work[:, size:] = contract(square, square, 1, 0)
    normalise(work)
    result = work[:, size:]
    miss = near_contract(result, result, 1, 1) - jnp.where(row == column, 1.0, 0.0)
    half = jnp.where(row > column, miss, jnp.where(row == column, 0.5 * miss, 0.0))
    rotation[...] = result - jnp.dot(
        half.astype(jnp.bfloat16), result.astype(jnp.bfloat16), preferred_element_type=jnp.float32
    )
    sound = jnp.sum(miss * miss) < 1e-2

    @pl.when(jnp.logical_not(sound))
    def _():
        work[:, size:] = gram[...]

        def step(iteration, carry):
            normalise(work)
            rotation[...] = work[:, size:]
            work[:, size:] = contract(rotation[...], gram[...], 1, 0)
            return carry

        lax.fori_loop(0, ITERS, step, 0)

    turned = rotation[...]
    turned_half = turned.astype(jnp.bfloat16)
    loading.wait()
    parts = store.shape[0]
    height = rows.shape[0] // parts
    storing = []
    for part in range(parts):
        span = pl.ds(part * height, height)
        rows[span, :] = lax.dot_general(
            prior[span, :], turned_half, (((1,), (1,)), ((), ())), preferred_element_type=jnp.float32
        ).astype(jnp.bfloat16)
        copy = pltpu.make_async_copy(rows.at[span], rows_hbm.at[span], store.at[part])
        copy.start()
        storing.append(copy)
    coords_ref[...] = near_contract(share_ref[...], turned, 1, 1)
    energy = turned * near_contract(turned, gram[...], 1, 0)
    total = near_contract(jnp.ones((16, size), jnp.float32), energy, 1, 1)
    singular_ref[...] = jnp.sqrt(total[:1])
    for copy in storing:
        copy.wait()


def all_to_all(pieces, axes):
    return lax.all_to_all(pieces, axes, 0, 0, tiled=True)


def repeat(piece, count):
    return jnp.broadcast_to(piece[None], (count,) + piece.shape)


def swap_cores(array):
    return lax.ppermute(array, "core", [(0, 1), (1, 0)])


def finish(packed, prior_sv, share_rows, basis_rows):
    height, rank_size = basis_rows.shape
    parts = 4
    return pl.pallas_call(
        rotate,
        in_specs=[pl.BlockSpec(memory_space=pltpu.VMEM)] * 3 + [pl.BlockSpec(memory_space=pl.ANY)],
        out_specs=(
            pl.BlockSpec(memory_space=pltpu.VMEM),
            pl.BlockSpec(memory_space=pl.ANY),
            pl.BlockSpec(memory_space=pltpu.VMEM),
        ),
        out_shape=(
            jax.ShapeDtypeStruct(share_rows.shape, jnp.float32),
            jax.ShapeDtypeStruct((height, rank_size), jnp.bfloat16),
            jax.ShapeDtypeStruct((1, rank_size), jnp.float32),
        ),
        scratch_shapes=[
            pltpu.VMEM((rank_size, rank_size), jnp.float32),
            pltpu.VMEM((rank_size, 2 * rank_size), jnp.float32),
            pltpu.VMEM((rank_size, rank_size), jnp.float32),
            pltpu.VMEM((height, rank_size), jnp.bfloat16),
            pltpu.VMEM((height, rank_size), jnp.bfloat16),
            pltpu.SemaphoreType.DMA,
            pltpu.SemaphoreType.DMA((parts,)),
        ],
        compiler_params=pltpu.CompilerParams(vmem_limit_bytes=32 * 2**20),
    )(packed, prior_sv.reshape(1, rank_size), share_rows, basis_rows)


def mass_pieces_kernel(slots, counts_ref, scale_ref, ids_ref, pieces_ref, mass):
    step = pl.program_id(0)
    width = counts_ref.shape[0] // slots
    docs = counts_ref.shape[1]
    doc_blocks = scale_ref.shape[0]
    marker = (
        lax.broadcasted_iota(jnp.int32, (16, docs), 1) // (docs // doc_blocks)
        == lax.broadcasted_iota(jnp.int32, (16, docs), 0)
    ).astype(jnp.bfloat16)
    for slot in range(slots):
        block = counts_ref[slot * width : (slot + 1) * width, :]
        sums = lax.dot_general(
            marker, block, (((1,), (1,)), ((), ())), preferred_element_type=jnp.float32
        )
        place = step * slots + slot
        total = sums[0:1] * scale_ref[0, place]
        for j in range(1, doc_blocks):
            total = total + sums[j : j + 1] * scale_ref[j, place]
        mass[pl.ds(place, 1), :] = total

    @pl.when(step == pl.num_programs(0) - 1)
    def _():
        stored = mass.shape[0]
        even = jnp.concatenate([mass[q : q + 1, :] for q in range(0, stored, 2)], axis=0)
        odd = jnp.concatenate([mass[q : q + 1, :] for q in range(1, stored, 2)], axis=0)
        half = LANES // 2
        lower = lax.broadcasted_iota(jnp.int32, even.shape, 1) < half
        near = jnp.where(lower, even, pltpu.roll(odd, half, 1))
        far = jnp.where(lower, pltpu.roll(even, half, 1), odd)
        ids = jnp.concatenate(
            [ids_ref[...].astype(jnp.float32), jnp.full((1, LANES - stored), -1.0, jnp.float32)], axis=1
        )
        period = jnp.concatenate([near, ids, far, ids] * 4, axis=0)
        rows = period.shape[0]
        for part in range(pieces_ref.shape[0] // rows):
            pieces_ref[part * rows : (part + 1) * rows, :] = period


def mass_pieces(counts, scales, block_ids, doc_count):
    height, docs = counts.shape
    stored = block_ids.shape[0]
    steps = 2
    return pl.pallas_call(
        functools.partial(mass_pieces_kernel, stored // steps),
        grid=(steps,),
        in_specs=[
            pl.BlockSpec((height // steps, docs), lambda i: (i, 0)),
            pl.BlockSpec(memory_space=pltpu.SMEM),
            pl.BlockSpec((1, stored), lambda i: (0, 0)),
        ],
        out_specs=pl.BlockSpec((doc_count * (stored // 2 + 1), LANES), lambda i: (0, 0)),
        out_shape=jax.ShapeDtypeStruct((doc_count * (stored // 2 + 1), LANES), jnp.float32),
        scratch_shapes=[pltpu.VMEM((stored, height // stored), jnp.float32)],
        compiler_params=pltpu.CompilerParams(vmem_limit_bytes=56 * 2**20),
    )(counts, scales.T, block_ids.reshape(1, stored))


def turn_kernel(after_ref, counts_ref, turned_ref):
    turned_ref[...] = counts_ref[...].T


def turn(counts, after):
    height, docs = counts.shape
    steps = 4
    return pl.pallas_call(
        turn_kernel,
        grid=(steps,),
        in_specs=[
            pl.BlockSpec(memory_space=pl.ANY),
            pl.BlockSpec((height // steps, docs), lambda i: (i, 0)),
        ],
        out_specs=pl.BlockSpec((docs, height // steps), lambda i: (0, i)),
        out_shape=jax.ShapeDtypeStruct((docs, height), counts.dtype),
        compiler_params=pltpu.CompilerParams(vmem_limit_bytes=6 * 2**20),
        cost_estimate=pl.CostEstimate(
            flops=0, bytes_accessed=4 * height * docs, transcendentals=0
        ),
    )(after, counts)


def find_masses_kernel(stored, place_ref, incoming_ref, before_ref, keep_ref, send_ref):
    piece = stored // 2 + 1
    batches = incoming_ref.shape[0] // piece
    half = LANES // 2
    chip, core = place_ref[0], place_ref[1]
    ids = incoming_ref[pl.ds(piece - 1, batches, stride=piece), :].T[:stored]
    batch = lax.broadcasted_iota(jnp.int32, ids.shape, 1)
    pair = [
        jnp.sum(jnp.where(batch == 2 * chip + side, ids, 0.0), axis=1, keepdims=True)
        for side in (0, 1)
    ]
    wanted = jnp.broadcast_to(jnp.concatenate(pair, axis=0), (2 * stored, batches))
    matches, parts = [], [[], [], []]
    for row in range(piece - 1):
        masses = incoming_ref[pl.ds(row, batches, stride=piece), :]
        high = masses.astype(jnp.bfloat16)
        rest = masses - high.astype(jnp.float32)
        low = rest.astype(jnp.bfloat16)
        last = (rest - low.astype(jnp.float32)).astype(jnp.bfloat16)
        for part, value in zip(parts, (high, low, last)):
            part.append(value)
        match = [
            jnp.where(wanted == ids[2 * row + slot : 2 * row + slot + 1], 1.0, 0.0)
            for slot in range(2)
        ]
        matches.append(jnp.concatenate(match, axis=0).astype(jnp.bfloat16))
    matches = jnp.concatenate(matches, axis=1)
    found = 0.0
    for part in parts:
        found = found + jnp.dot(
            matches, jnp.concatenate(part, axis=0), preferred_element_type=jnp.float32
        )
    masses = found[: 2 * stored, :half] + found[2 * stored :, half:]
    mine = core == 0
    keep_ref[...] = jnp.where(mine, masses[:stored], masses[stored:])
    send_ref[...] = jnp.where(mine, masses[stored:], masses[:stored])


def find_masses(incoming, before, chip, core, stored):
    shape = jax.ShapeDtypeStruct((stored, LANES // 2), jnp.float32)
    return pl.pallas_call(
        functools.partial(find_masses_kernel, stored),
        in_specs=[
            pl.BlockSpec(memory_space=pltpu.SMEM),
            pl.BlockSpec(memory_space=pltpu.VMEM),
            pl.BlockSpec(memory_space=pl.ANY),
        ],
        out_specs=(pl.BlockSpec(memory_space=pltpu.VMEM), pl.BlockSpec(memory_space=pltpu.VMEM)),
        out_shape=(shape, shape),
        compiler_params=pltpu.CompilerParams(vmem_limit_bytes=6 * 2**20),
    )(jnp.stack([chip, core]).astype(jnp.int32), incoming, before)


def project_kernel(
    total_docs, core_ref, keep_ref, come_ref, scale_ref, prior_ref, turned_ref, partial_ref, basis
):
    stored = keep_ref.shape[0]
    doc_blocks = scale_ref.shape[0]
    height = prior_ref.shape[0]
    width = height // stored
    docs = partial_ref.shape[0] // doc_blocks
    mine, other = keep_ref[...], come_ref[...]
    first = core_ref[0] == 0
    term_mass = jnp.concatenate(
        [jnp.where(first, mine, other), jnp.where(first, other, mine)], axis=1
    )
    weight = jnp.log(1.0 + total_docs / (1.0 + term_mass))
    spare = jnp.zeros((LANES - stored, LANES), jnp.float32)
    turned_weight = jnp.concatenate([weight, spare], axis=0).T[:, :stored]
    columns = [turned_weight * scale_ref[j : j + 1, :] / math.sqrt(TERMS) for j in range(doc_blocks)]
    for block in range(stored):
        span = slice(block * width, (block + 1) * width)
        prior = prior_ref[span, :].astype(jnp.float32)
        for j in range(doc_blocks):
            basis[j, span, :] = (prior * columns[j][:, block : block + 1]).astype(jnp.bfloat16)
    for j in range(doc_blocks):
        partial_ref[j * docs : (j + 1) * docs, :] = jnp.dot(
            turned_ref[j * docs : (j + 1) * docs, :], basis[j], preferred_element_type=jnp.float32
        )


def project(core, keep, come, scales, prior, turned, total_docs):
    height, rank_size = prior.shape
    docs = turned.shape[0]
    doc_blocks = scales.shape[1]
    vmem = pl.BlockSpec(memory_space=pltpu.VMEM)
    return pl.pallas_call(
        functools.partial(project_kernel, total_docs),
        in_specs=[pl.BlockSpec(memory_space=pltpu.SMEM)] + [vmem] * 5,
        out_specs=vmem,
        out_shape=jax.ShapeDtypeStruct((docs, rank_size), jnp.float32),
        scratch_shapes=[pltpu.VMEM((doc_blocks, height, rank_size), jnp.bfloat16)],
        compiler_params=pltpu.CompilerParams(vmem_limit_bytes=32 * 2**20),
    )(core.reshape(1).astype(jnp.int32), keep, come, scales.T, prior, turned)


def shards(tf_blocks, block_scale, term_blocks, prior_rows, prior_sv):
    counts = tf_blocks[0]
    scales = block_scale[0]
    block_ids = term_blocks[0]
    basis_rows = prior_rows[0]
    stored_blocks = block_ids.shape[0]
    batch_docs = counts.shape[1]
    rank_size = basis_rows.shape[1]
    planes, lines = lax.axis_size("z"), lax.axis_size("y")
    doc_count = planes * lines * lax.axis_size("core")
    term_count = lax.axis_size("term")
    total_docs = batch_docs * doc_count
    share_docs = batch_docs // term_count
    pieces = mass_pieces(counts, scales, block_ids, doc_count)
    incoming = all_to_all(pieces.reshape(doc_count, 1, -1), ("z", "y", "core"))
    turned = turn(counts, pieces[:8])
    chip = lax.axis_index("z") * lines + lax.axis_index("y")
    core = lax.axis_index("core")
    keep, send = find_masses(incoming.reshape(-1, LANES), turned, chip, core, stored_blocks)
    come = swap_cores(send)
    partial = project(core, keep, come, scales, basis_rows, turned, total_docs)
    partial = partial.reshape(term_count, share_docs, rank_size)
    share_rows, packed = own_gram(all_to_all(partial, "term"), total_docs)
    plane = ("y", "term")
    across = ("z", "core")
    plane_count = lines * term_count
    plane_gram = jnp.sum(all_to_all(packed.reshape(plane_count, 1, -1), plane), axis=0)
    piece_gram = jnp.sum(all_to_all(repeat(plane_gram, doc_count // lines), across), axis=0)
    packed = all_to_all(repeat(piece_gram, plane_count), plane).reshape(-1, LANES)
    doc_coords, new_rows, singular = finish(packed, prior_sv, share_rows, basis_rows)
    return (doc_coords, new_rows[None], singular.reshape(rank_size))


def solution(mesh):
    planes = lines = 8
    named = Mesh(
        mesh.devices.reshape(planes, lines, -1, mesh.shape["term"]), ("z", "y", "core", "term")
    )
    doc = ("z", "y", "core")
    in_specs = (
        P(doc, "term", None),
        P(doc, "term", None),
        P(doc, "term"),
        P(doc, "term", None),
        P(),
    )
    out_specs = (P(doc + ("term",), None), P(doc, "term", None), P())
    return jax.shard_map(shards, mesh=named, in_specs=in_specs, out_specs=out_specs, check_vma=False)
```

```python
import functools
import math

import jax
import jax.numpy as jnp
from jax import lax
from jax.experimental import pallas as pl
from jax.experimental.pallas import tpu as pltpu
from jax.sharding import Mesh
from jax.sharding import PartitionSpec as P

TERMS = 131072
ITERS = 4
LANES = 128
PANEL = 32
HALF = 16


forget_factor = 0.85
highest = lax.Precision.HIGHEST


def contract(a, b, a_dim, b_dim):
    return lax.dot_general(
        a,
        b,
        (((a_dim,), (b_dim,)), ((), ())),
        precision=highest,
        preferred_element_type=jnp.float32,
    )


def eliminate(panel, first):
    height = panel.shape[0]
    rows = lax.broadcasted_iota(jnp.int32, (HALF, LANES), 0)
    parts = [
        [panel[top : top + HALF, t : t + LANES] for t in range(0, panel.shape[1], LANES)]
        for top in range(0, height, HALF)
    ]
    done = []
    while parts:
        lead, *below = parts
        start = first + len(done) * HALF
        tile, lane = start // LANES, start % LANES
        columns = [
            [jnp.broadcast_to(part[tile][:, lane + k : lane + k + 1], (HALF, LANES)) for k in range(HALF)]
            for part in parts
        ]
        pivots = jnp.zeros((HALF, LANES), jnp.float32)
        for k in range(HALF):
            pivot = columns[0][k][k : k + 1, :]
            pivots = jnp.where(rows == k, jnp.broadcast_to(pivot, (HALF, LANES)), pivots)
            unit = 1.0 / pivot
            factors = [jnp.where(rows > k, columns[0][k] * unit, 0.0)]
            factors += [column[k] * unit for column in columns[1:]]
            for m in range(k + 1, HALF):
                value = columns[0][m][k : k + 1, :]
                for column, factor in zip(columns, factors):
                    column[m] = column[m] - factor * value
            values = [entry[k : k + 1, :] for entry in lead]
            lead = [entry - factors[0] * value for entry, value in zip(lead, values)]
            below = [
                [entry - factor * value for entry, value in zip(part, values)]
                for part, factor in zip(below, factors[1:])
            ]
        root = lax.rsqrt(pivots)
        done.append(jnp.concatenate([entry * root for entry in lead], axis=1))
        parts = below
    return jnp.concatenate(done, axis=0)


def split(value):
    high = value.astype(jnp.bfloat16)
    rest = value - high.astype(jnp.float32)
    middle = rest.astype(jnp.bfloat16)
    return high, middle, (rest - middle.astype(jnp.float32)).astype(jnp.bfloat16)


def fold(rows, second):
    high, middle, low = split(rows)
    right = jnp.concatenate([high, middle, high, middle, low, high], axis=0)
    left = jnp.concatenate([high, high, middle, middle, high, low], axis=0)
    return lax.dot_general(
        left[:, second : second + PANEL],
        right,
        (((0,), (0,)), ((), ())),
        preferred_element_type=jnp.float32,
    )


def orthonormal_rows(work):
    size = work.shape[0]
    panel = work[:PANEL, :]
    for first in range(0, size, PANEL):
        second = first + PANEL
        left, later = first // LANES * LANES, second // LANES * LANES
        if second < size:
            ahead = work[second : second + PANEL, later:]
            if first > 0:
                ahead = ahead - contract(
                    work[:first, second : second + PANEL], work[:first, later:], 0, 0
                )
        rows = eliminate(panel, first - left)
        work[first:second, left:] = rows
        if second < size:
            panel = ahead - fold(rows[:, later - left :], second - later)


def normalise(work):
    size = work.shape[0]
    image = work[:, size:]
    work[:, :size] = contract(image, image, 1, 1)
    orthonormal_rows(work)


def pack(matrix):
    half = LANES // 2
    lower = lax.broadcasted_iota(jnp.int32, (half, LANES), 1) < half
    inner = pltpu.roll(matrix[half:LANES, :LANES], half, 1)
    corner = matrix[LANES + half :, LANES:]
    return jnp.concatenate(
        [
            matrix[:half, :LANES],
            matrix[:half, LANES:],
            matrix[half:LANES, LANES:],
            matrix[LANES : LANES + half, LANES:],
            jnp.where(lower, inner, corner),
        ],
        axis=0,
    )


def unpack(packed):
    half = LANES // 2
    blocks = [packed[top : top + half] for top in range(0, packed.shape[0], half)]
    spare = jnp.zeros((half, LANES), jnp.float32)
    left = jnp.concatenate([blocks[0], pltpu.roll(blocks[4], half, 1), spare, spare], axis=0)
    right = jnp.concatenate([blocks[1], blocks[2], blocks[3], blocks[4]], axis=0)
    upper = jnp.concatenate([left, right], axis=1)
    row = lax.broadcasted_iota(jnp.int32, upper.shape, 0) // half
    column = lax.broadcasted_iota(jnp.int32, upper.shape, 1) // half
    return jnp.where(row <= column, upper, upper.T)


def own_gram_kernel(total_docs, incoming_ref, share_ref, packed_ref):
    share = jnp.sum(incoming_ref[...], axis=0)
    share_ref[...] = share
    packed_ref[...] = pack(contract(share, share, 0, 0) * (1.0 / total_docs))


def own_gram(incoming, total_docs):
    docs, rank_size = incoming.shape[1:]
    vmem = pl.BlockSpec(memory_space=pltpu.VMEM)
    return pl.pallas_call(
        functools.partial(own_gram_kernel, total_docs),
        in_specs=[vmem],
        out_specs=(vmem, vmem),
        out_shape=(
            jax.ShapeDtypeStruct((docs, rank_size), jnp.float32),
            jax.ShapeDtypeStruct((5 * LANES // 2, LANES), jnp.float32),
        ),
        compiler_params=pltpu.CompilerParams(vmem_limit_bytes=8 * 2**20),
    )(incoming)


def near_contract(a, b, a_dim, b_dim):
    def halves(value):
        high = value.astype(jnp.bfloat16)
        return high, (value - high.astype(jnp.float32)).astype(jnp.bfloat16)

    (a_high, a_low), (b_high, b_low) = halves(a), halves(b)
    return lax.dot_general(
        jnp.concatenate([a_high, a_high, a_low], axis=a_dim),
        jnp.concatenate([b_high, b_low, b_high], axis=b_dim),
        (((a_dim,), (b_dim,)), ((), ())),
        preferred_element_type=jnp.float32,
    )


def rotate(
    packed_ref, sv_ref, share_ref, prior_hbm,
    coords_ref, rows_hbm, singular_ref,
    gram, work, rotation, prior, rows, load, store,
):
    loading = pltpu.make_async_copy(prior_hbm, prior, load)
    loading.start()
    size = sv_ref.shape[1]
    row = lax.broadcasted_iota(jnp.int32, (size, size), 0)
    column = lax.broadcasted_iota(jnp.int32, (size, size), 1)
    sv = sv_ref[...]
    whole = unpack(packed_ref[...]) + jnp.where(row == column, forget_factor * sv * sv, 0.0)
    gram[...] = whole
    diagonal = jnp.where(row == column, whole, 0.0)
    top = jnp.max(jnp.max(diagonal, axis=0, keepdims=True), axis=1, keepdims=True)
    scaled = whole * (1.0 / top)
    square = contract(scaled, scaled, 1, 0)
    work[:, size:] = contract(square, square, 1, 0)
    normalise(work)
    result = work[:, size:]
    miss = near_contract(result, result, 1, 1) - jnp.where(row == column, 1.0, 0.0)
    half = jnp.where(row > column, miss, jnp.where(row == column, 0.5 * miss, 0.0))
    rotation[...] = result - jnp.dot(
        half.astype(jnp.bfloat16), result.astype(jnp.bfloat16), preferred_element_type=jnp.float32
    )
    sound = jnp.sum(miss * miss) < 1e-2

    @pl.when(jnp.logical_not(sound))
    def _():
        work[:, size:] = gram[...]

        def step(iteration, carry):
            normalise(work)
            rotation[...] = work[:, size:]
            work[:, size:] = contract(rotation[...], gram[...], 1, 0)
            return carry

        lax.fori_loop(0, ITERS, step, 0)

    turned = rotation[...]
    turned_half = turned.astype(jnp.bfloat16)
    loading.wait()
    parts = store.shape[0]
    height = rows.shape[0] // parts
    storing = []
    for part in range(parts):
        span = pl.ds(part * height, height)
        rows[span, :] = lax.dot_general(
            prior[span, :], turned_half, (((1,), (1,)), ((), ())), preferred_element_type=jnp.float32
        ).astype(jnp.bfloat16)
        copy = pltpu.make_async_copy(rows.at[span], rows_hbm.at[span], store.at[part])
        copy.start()
        storing.append(copy)
    coords_ref[...] = near_contract(share_ref[...], turned, 1, 1)
    energy = turned * near_contract(turned, gram[...], 1, 0)
    total = near_contract(jnp.ones((16, size), jnp.float32), energy, 1, 1)
    singular_ref[...] = jnp.sqrt(total[:1])
    for copy in storing:
        copy.wait()


def all_to_all(pieces, axes):
    return lax.all_to_all(pieces, axes, 0, 0, tiled=True)


def repeat(piece, count):
    return jnp.broadcast_to(piece[None], (count,) + piece.shape)


def swap_cores(array):
    both = lax.all_gather(array, "core", axis=0)
    return jnp.where(lax.axis_index("core") == 0, both[1], both[0])


def finish(packed, prior_sv, share_rows, basis_rows):
    height, rank_size = basis_rows.shape
    parts = 4
    return pl.pallas_call(
        rotate,
        in_specs=[pl.BlockSpec(memory_space=pltpu.VMEM)] * 3 + [pl.BlockSpec(memory_space=pl.ANY)],
        out_specs=(
            pl.BlockSpec(memory_space=pltpu.VMEM),
            pl.BlockSpec(memory_space=pl.ANY),
            pl.BlockSpec(memory_space=pltpu.VMEM),
        ),
        out_shape=(
            jax.ShapeDtypeStruct(share_rows.shape, jnp.float32),
            jax.ShapeDtypeStruct((height, rank_size), jnp.bfloat16),
            jax.ShapeDtypeStruct((1, rank_size), jnp.float32),
        ),
        scratch_shapes=[
            pltpu.VMEM((rank_size, rank_size), jnp.float32),
            pltpu.VMEM((rank_size, 2 * rank_size), jnp.float32),
            pltpu.VMEM((rank_size, rank_size), jnp.float32),
            pltpu.VMEM((height, rank_size), jnp.bfloat16),
            pltpu.VMEM((height, rank_size), jnp.bfloat16),
            pltpu.SemaphoreType.DMA,
            pltpu.SemaphoreType.DMA((parts,)),
        ],
        compiler_params=pltpu.CompilerParams(vmem_limit_bytes=32 * 2**20),
    )(packed, prior_sv.reshape(1, rank_size), share_rows, basis_rows)


def mass_pieces_kernel(slots, counts_ref, scale_ref, ids_ref, pieces_ref, mass):
    step = pl.program_id(0)
    width = counts_ref.shape[0] // slots
    docs = counts_ref.shape[1]
    doc_blocks = scale_ref.shape[0]
    marker = (
        lax.broadcasted_iota(jnp.int32, (16, docs), 1) // (docs // doc_blocks)
        == lax.broadcasted_iota(jnp.int32, (16, docs), 0)
    ).astype(jnp.bfloat16)
    for slot in range(slots):
        block = counts_ref[slot * width : (slot + 1) * width, :]
        sums = lax.dot_general(
            marker, block, (((1,), (1,)), ((), ())), preferred_element_type=jnp.float32
        )
        place = step * slots + slot
        total = sums[0:1] * scale_ref[0, place]
        for j in range(1, doc_blocks):
            total = total + sums[j : j + 1] * scale_ref[j, place]
        mass[pl.ds(place, 1), :] = total

    @pl.when(step == pl.num_programs(0) - 1)
    def _():
        stored = mass.shape[0]
        even = jnp.concatenate([mass[q : q + 1, :] for q in range(0, stored, 2)], axis=0)
        odd = jnp.concatenate([mass[q : q + 1, :] for q in range(1, stored, 2)], axis=0)
        half = LANES // 2
        lower = lax.broadcasted_iota(jnp.int32, even.shape, 1) < half
        near = jnp.where(lower, even, pltpu.roll(odd, half, 1))
        far = jnp.where(lower, pltpu.roll(even, half, 1), odd)
        ids = jnp.concatenate(
            [ids_ref[...].astype(jnp.float32), jnp.full((1, LANES - stored), -1.0, jnp.float32)], axis=1
        )
        period = jnp.concatenate([near, ids, far, ids] * 4, axis=0)
        rows = period.shape[0]
        for part in range(pieces_ref.shape[0] // rows):
            pieces_ref[part * rows : (part + 1) * rows, :] = period


def mass_pieces(counts, scales, block_ids, doc_count):
    height, docs = counts.shape
    stored = block_ids.shape[0]
    steps = 2
    return pl.pallas_call(
        functools.partial(mass_pieces_kernel, stored // steps),
        grid=(steps,),
        in_specs=[
            pl.BlockSpec((height // steps, docs), lambda i: (i, 0)),
            pl.BlockSpec(memory_space=pltpu.SMEM),
            pl.BlockSpec((1, stored), lambda i: (0, 0)),
        ],
        out_specs=pl.BlockSpec((doc_count * (stored // 2 + 1), LANES), lambda i: (0, 0)),
        out_shape=jax.ShapeDtypeStruct((doc_count * (stored // 2 + 1), LANES), jnp.float32),
        scratch_shapes=[pltpu.VMEM((stored, height // stored), jnp.float32)],
        compiler_params=pltpu.CompilerParams(vmem_limit_bytes=56 * 2**20),
    )(counts, scales.T, block_ids.reshape(1, stored))


def turn_kernel(after_ref, counts_ref, turned_ref):
    turned_ref[...] = counts_ref[...].T


def turn(counts, after):
    height, docs = counts.shape
    steps = 4
    return pl.pallas_call(
        turn_kernel,
        grid=(steps,),
        in_specs=[
            pl.BlockSpec(memory_space=pl.ANY),
            pl.BlockSpec((height // steps, docs), lambda i: (i, 0)),
        ],
        out_specs=pl.BlockSpec((docs, height // steps), lambda i: (0, i)),
        out_shape=jax.ShapeDtypeStruct((docs, height), counts.dtype),
        compiler_params=pltpu.CompilerParams(vmem_limit_bytes=6 * 2**20),
        cost_estimate=pl.CostEstimate(
            flops=0, bytes_accessed=4 * height * docs, transcendentals=0
        ),
    )(after, counts)


def find_masses_kernel(stored, place_ref, incoming_ref, before_ref, keep_ref, send_ref):
    piece = stored // 2 + 1
    batches = incoming_ref.shape[0] // piece
    half = LANES // 2
    chip, core = place_ref[0], place_ref[1]
    ids = incoming_ref[pl.ds(piece - 1, batches, stride=piece), :].T[:stored]
    batch = lax.broadcasted_iota(jnp.int32, ids.shape, 1)
    pair = [
        jnp.sum(jnp.where(batch == 2 * chip + side, ids, 0.0), axis=1, keepdims=True)
        for side in (0, 1)
    ]
    wanted = jnp.broadcast_to(jnp.concatenate(pair, axis=0), (2 * stored, batches))
    matches, parts = [], [[], [], []]
    for row in range(piece - 1):
        masses = incoming_ref[pl.ds(row, batches, stride=piece), :]
        high = masses.astype(jnp.bfloat16)
        rest = masses - high.astype(jnp.float32)
        low = rest.astype(jnp.bfloat16)
        last = (rest - low.astype(jnp.float32)).astype(jnp.bfloat16)
        for part, value in zip(parts, (high, low, last)):
            part.append(value)
        match = [
            jnp.where(wanted == ids[2 * row + slot : 2 * row + slot + 1], 1.0, 0.0)
            for slot in range(2)
        ]
        matches.append(jnp.concatenate(match, axis=0).astype(jnp.bfloat16))
    matches = jnp.concatenate(matches, axis=1)
    found = 0.0
    for part in parts:
        found = found + jnp.dot(
            matches, jnp.concatenate(part, axis=0), preferred_element_type=jnp.float32
        )
    masses = found[: 2 * stored, :half] + found[2 * stored :, half:]
    mine = core == 0
    keep_ref[...] = jnp.where(mine, masses[:stored], masses[stored:])
    send_ref[...] = jnp.where(mine, masses[stored:], masses[:stored])


def find_masses(incoming, before, chip, core, stored):
    shape = jax.ShapeDtypeStruct((stored, LANES // 2), jnp.float32)
    return pl.pallas_call(
        functools.partial(find_masses_kernel, stored),
        in_specs=[
            pl.BlockSpec(memory_space=pltpu.SMEM),
            pl.BlockSpec(memory_space=pltpu.VMEM),
            pl.BlockSpec(memory_space=pl.ANY),
        ],
        out_specs=(pl.BlockSpec(memory_space=pltpu.VMEM), pl.BlockSpec(memory_space=pltpu.VMEM)),
        out_shape=(shape, shape),
        compiler_params=pltpu.CompilerParams(vmem_limit_bytes=6 * 2**20),
    )(jnp.stack([chip, core]).astype(jnp.int32), incoming, before)


def project_kernel(
    total_docs, core_ref, keep_ref, come_ref, scale_ref, prior_ref, turned_ref, partial_ref, basis
):
    stored = keep_ref.shape[0]
    doc_blocks = scale_ref.shape[0]
    height = prior_ref.shape[0]
    width = height // stored
    docs = partial_ref.shape[0] // doc_blocks
    mine, other = keep_ref[...], come_ref[...]
    first = core_ref[0] == 0
    term_mass = jnp.concatenate(
        [jnp.where(first, mine, other), jnp.where(first, other, mine)], axis=1
    )
    weight = jnp.log(1.0 + total_docs / (1.0 + term_mass))
    spare = jnp.zeros((LANES - stored, LANES), jnp.float32)
    turned_weight = jnp.concatenate([weight, spare], axis=0).T[:, :stored]
    columns = [turned_weight * scale_ref[j : j + 1, :] / math.sqrt(TERMS) for j in range(doc_blocks)]
    for block in range(stored):
        span = slice(block * width, (block + 1) * width)
        prior = prior_ref[span, :].astype(jnp.float32)
        for j in range(doc_blocks):
            basis[j, span, :] = (prior * columns[j][:, block : block + 1]).astype(jnp.bfloat16)
    for j in range(doc_blocks):
        partial_ref[j * docs : (j + 1) * docs, :] = jnp.dot(
            turned_ref[j * docs : (j + 1) * docs, :], basis[j], preferred_element_type=jnp.float32
        )


def project(core, keep, come, scales, prior, turned, total_docs):
    height, rank_size = prior.shape
    docs = turned.shape[0]
    doc_blocks = scales.shape[1]
    vmem = pl.BlockSpec(memory_space=pltpu.VMEM)
    return pl.pallas_call(
        functools.partial(project_kernel, total_docs),
        in_specs=[pl.BlockSpec(memory_space=pltpu.SMEM)] + [vmem] * 5,
        out_specs=vmem,
        out_shape=jax.ShapeDtypeStruct((docs, rank_size), jnp.float32),
        scratch_shapes=[pltpu.VMEM((doc_blocks, height, rank_size), jnp.bfloat16)],
        compiler_params=pltpu.CompilerParams(vmem_limit_bytes=32 * 2**20),
    )(core.reshape(1).astype(jnp.int32), keep, come, scales.T, prior, turned)


def shards(tf_blocks, block_scale, term_blocks, prior_rows, prior_sv):
    counts = tf_blocks[0]
    scales = block_scale[0]
    block_ids = term_blocks[0]
    basis_rows = prior_rows[0]
    stored_blocks = block_ids.shape[0]
    batch_docs = counts.shape[1]
    rank_size = basis_rows.shape[1]
    planes, lines = lax.axis_size("z"), lax.axis_size("y")
    doc_count = planes * lines * lax.axis_size("core")
    term_count = lax.axis_size("term")
    total_docs = batch_docs * doc_count
    share_docs = batch_docs // term_count
    pieces = mass_pieces(counts, scales, block_ids, doc_count)
    incoming = all_to_all(pieces.reshape(doc_count, 1, -1), ("z", "y", "core"))
    turned = turn(counts, pieces[:8])
    chip = lax.axis_index("z") * lines + lax.axis_index("y")
    core = lax.axis_index("core")
    keep, send = find_masses(incoming.reshape(-1, LANES), turned, chip, core, stored_blocks)
    come = swap_cores(send)
    partial = project(core, keep, come, scales, basis_rows, turned, total_docs)
    partial = partial.reshape(term_count, share_docs, rank_size)
    share_rows, packed = own_gram(all_to_all(partial, "term"), total_docs)
    plane = ("y", "term")
    across = ("z", "core")
    plane_count = lines * term_count
    plane_gram = jnp.sum(all_to_all(packed.reshape(plane_count, 1, -1), plane), axis=0)
    piece_gram = jnp.sum(all_to_all(repeat(plane_gram, doc_count // lines), across), axis=0)
    packed = all_to_all(repeat(piece_gram, plane_count), plane).reshape(-1, LANES)
    doc_coords, new_rows, singular = finish(packed, prior_sv, share_rows, basis_rows)
    return (doc_coords, new_rows[None], singular.reshape(rank_size))


def solution(mesh):
    planes = lines = 8
    named = Mesh(
        mesh.devices.reshape(planes, lines, -1, mesh.shape["term"]), ("z", "y", "core", "term")
    )
    doc = ("z", "y", "core")
    in_specs = (
        P(doc, "term", None),
        P(doc, "term", None),
        P(doc, "term"),
        P(doc, "term", None),
        P(),
    )
    out_specs = (P(doc + ("term",), None), P(doc, "term", None), P())
    return jax.shard_map(shards, mesh=named, in_specs=in_specs, out_specs=out_specs, check_vma=False)
```

```python
import functools
import math

import jax
import jax.numpy as jnp
from jax import lax
from jax.experimental import pallas as pl
from jax.experimental.pallas import tpu as pltpu
from jax.sharding import Mesh
from jax.sharding import PartitionSpec as P

TERMS = 131072
ITERS = 4
LANES = 128
PANEL = 32
HALF = 16


forget_factor = 0.85
highest = lax.Precision.HIGHEST


def contract(a, b, a_dim, b_dim):
    return lax.dot_general(
        a,
        b,
        (((a_dim,), (b_dim,)), ((), ())),
        precision=highest,
        preferred_element_type=jnp.float32,
    )


def eliminate(panel, first):
    height = panel.shape[0]
    rows = lax.broadcasted_iota(jnp.int32, (HALF, LANES), 0)
    parts = [
        [panel[top : top + HALF, t : t + LANES] for t in range(0, panel.shape[1], LANES)]
        for top in range(0, height, HALF)
    ]
    done = []
    while parts:
        lead, *below = parts
        start = first + len(done) * HALF
        tile, lane = start // LANES, start % LANES
        columns = [
            [jnp.broadcast_to(part[tile][:, lane + k : lane + k + 1], (HALF, LANES)) for k in range(HALF)]
            for part in parts
        ]
        pivots = jnp.zeros((HALF, LANES), jnp.float32)
        for k in range(HALF):
            pivot = columns[0][k][k : k + 1, :]
            pivots = jnp.where(rows == k, jnp.broadcast_to(pivot, (HALF, LANES)), pivots)
            unit = 1.0 / pivot
            factors = [jnp.where(rows > k, columns[0][k] * unit, 0.0)]
            factors += [column[k] * unit for column in columns[1:]]
            for m in range(k + 1, HALF):
                value = columns[0][m][k : k + 1, :]
                for column, factor in zip(columns, factors):
                    column[m] = column[m] - factor * value
            values = [entry[k : k + 1, :] for entry in lead]
            lead = [entry - factors[0] * value for entry, value in zip(lead, values)]
            below = [
                [entry - factor * value for entry, value in zip(part, values)]
                for part, factor in zip(below, factors[1:])
            ]
        root = lax.rsqrt(pivots)
        done.append(jnp.concatenate([entry * root for entry in lead], axis=1))
        parts = below
    return jnp.concatenate(done, axis=0)


def split(value):
    high = value.astype(jnp.bfloat16)
    rest = value - high.astype(jnp.float32)
    middle = rest.astype(jnp.bfloat16)
    return high, middle, (rest - middle.astype(jnp.float32)).astype(jnp.bfloat16)


def fold(rows, second):
    high, middle, low = split(rows)
    right = jnp.concatenate([high, middle, high, middle, low, high], axis=0)
    left = jnp.concatenate([high, high, middle, middle, high, low], axis=0)
    return lax.dot_general(
        left[:, second : second + PANEL],
        right,
        (((0,), (0,)), ((), ())),
        preferred_element_type=jnp.float32,
    )


def orthonormal_rows(work):
    size = work.shape[0]
    panel = work[:PANEL, :]
    for first in range(0, size, PANEL):
        second = first + PANEL
        left, later = first // LANES * LANES, second // LANES * LANES
        if second < size:
            ahead = work[second : second + PANEL, later:]
            if first > 0:
                ahead = ahead - contract(
                    work[:first, second : second + PANEL], work[:first, later:], 0, 0
                )
        rows = eliminate(panel, first - left)
        work[first:second, left:] = rows
        if second < size:
            panel = ahead - fold(rows[:, later - left :], second - later)


def normalise(work):
    size = work.shape[0]
    image = work[:, size:]
    work[:, :size] = contract(image, image, 1, 1)
    orthonormal_rows(work)


def pack(matrix):
    half = LANES // 2
    lower = lax.broadcasted_iota(jnp.int32, (half, LANES), 1) < half
    inner = pltpu.roll(matrix[half:LANES, :LANES], half, 1)
    corner = matrix[LANES + half :, LANES:]
    return jnp.concatenate(
        [
            matrix[:half, :LANES],
            matrix[:half, LANES:],
            matrix[half:LANES, LANES:],
            matrix[LANES : LANES + half, LANES:],
            jnp.where(lower, inner, corner),
        ],
        axis=0,
    )


def unpack(packed):
    half = LANES // 2
    blocks = [packed[top : top + half] for top in range(0, packed.shape[0], half)]
    spare = jnp.zeros((half, LANES), jnp.float32)
    left = jnp.concatenate([blocks[0], pltpu.roll(blocks[4], half, 1), spare, spare], axis=0)
    right = jnp.concatenate([blocks[1], blocks[2], blocks[3], blocks[4]], axis=0)
    upper = jnp.concatenate([left, right], axis=1)
    row = lax.broadcasted_iota(jnp.int32, upper.shape, 0) // half
    column = lax.broadcasted_iota(jnp.int32, upper.shape, 1) // half
    return jnp.where(row <= column, upper, upper.T)


def own_gram_kernel(total_docs, incoming_ref, share_ref, packed_ref):
    share = jnp.sum(incoming_ref[...], axis=0)
    share_ref[...] = share
    packed_ref[...] = pack(contract(share, share, 0, 0) * (1.0 / total_docs))


def own_gram(incoming, total_docs):
    docs, rank_size = incoming.shape[1:]
    vmem = pl.BlockSpec(memory_space=pltpu.VMEM)
    return pl.pallas_call(
        functools.partial(own_gram_kernel, total_docs),
        in_specs=[vmem],
        out_specs=(vmem, vmem),
        out_shape=(
            jax.ShapeDtypeStruct((docs, rank_size), jnp.float32),
            jax.ShapeDtypeStruct((5 * LANES // 2, LANES), jnp.float32),
        ),
        compiler_params=pltpu.CompilerParams(vmem_limit_bytes=8 * 2**20),
    )(incoming)


def near_contract(a, b, a_dim, b_dim):
    def halves(value):
        high = value.astype(jnp.bfloat16)
        return high, (value - high.astype(jnp.float32)).astype(jnp.bfloat16)

    (a_high, a_low), (b_high, b_low) = halves(a), halves(b)
    return lax.dot_general(
        jnp.concatenate([a_high, a_high, a_low], axis=a_dim),
        jnp.concatenate([b_high, b_low, b_high], axis=b_dim),
        (((a_dim,), (b_dim,)), ((), ())),
        preferred_element_type=jnp.float32,
    )


def rotate(
    packed_ref, sv_ref, share_ref, prior_hbm,
    coords_ref, rows_hbm, singular_ref,
    gram, work, rotation, prior, rows, load, store,
):
    loading = pltpu.make_async_copy(prior_hbm, prior, load)
    loading.start()
    size = sv_ref.shape[1]
    row = lax.broadcasted_iota(jnp.int32, (size, size), 0)
    column = lax.broadcasted_iota(jnp.int32, (size, size), 1)
    sv = sv_ref[...]
    whole = unpack(packed_ref[...]) + jnp.where(row == column, forget_factor * sv * sv, 0.0)
    gram[...] = whole
    diagonal = jnp.where(row == column, whole, 0.0)
    top = jnp.max(jnp.max(diagonal, axis=0, keepdims=True), axis=1, keepdims=True)
    scaled = whole * (1.0 / top)
    square = contract(scaled, scaled, 1, 0)
    work[:, size:] = contract(square, square, 1, 0)
    normalise(work)
    result = work[:, size:]
    miss = near_contract(result, result, 1, 1) - jnp.where(row == column, 1.0, 0.0)
    half = jnp.where(row > column, miss, jnp.where(row == column, 0.5 * miss, 0.0))
    rotation[...] = result - jnp.dot(
        half.astype(jnp.bfloat16), result.astype(jnp.bfloat16), preferred_element_type=jnp.float32
    )
    sound = jnp.sum(miss * miss) < 1e-2

    @pl.when(jnp.logical_not(sound))
    def _():
        work[:, size:] = gram[...]

        def step(iteration, carry):
            normalise(work)
            rotation[...] = work[:, size:]
            work[:, size:] = contract(rotation[...], gram[...], 1, 0)
            return carry

        lax.fori_loop(0, ITERS, step, 0)

    turned = rotation[...]
    turned_half = turned.astype(jnp.bfloat16)
    loading.wait()
    parts = store.shape[0]
    height = rows.shape[0] // parts
    storing = []
    for part in range(parts):
        span = pl.ds(part * height, height)
        rows[span, :] = lax.dot_general(
            prior[span, :], turned_half, (((1,), (1,)), ((), ())), preferred_element_type=jnp.float32
        ).astype(jnp.bfloat16)
        copy = pltpu.make_async_copy(rows.at[span], rows_hbm.at[span], store.at[part])
        copy.start()
        storing.append(copy)
    coords_ref[...] = near_contract(share_ref[...], turned, 1, 1)
    energy = turned * near_contract(turned, gram[...], 1, 0)
    total = near_contract(jnp.ones((16, size), jnp.float32), energy, 1, 1)
    singular_ref[...] = jnp.sqrt(total[:1])
    for copy in storing:
        copy.wait()


def all_to_all(pieces, axes):
    return lax.all_to_all(pieces, axes, 0, 0, tiled=True)


def repeat(piece, count):
    return jnp.broadcast_to(piece[None], (count,) + piece.shape)


def swap_cores(array):
    both = lax.all_gather(array, "core", axis=0)
    return jnp.where(lax.axis_index("core") == 0, both[1], both[0])


def finish(packed, prior_sv, share_rows, basis_rows):
    height, rank_size = basis_rows.shape
    parts = 4
    return pl.pallas_call(
        rotate,
        in_specs=[pl.BlockSpec(memory_space=pltpu.VMEM)] * 3 + [pl.BlockSpec(memory_space=pl.ANY)],
        out_specs=(
            pl.BlockSpec(memory_space=pltpu.VMEM),
            pl.BlockSpec(memory_space=pl.ANY),
            pl.BlockSpec(memory_space=pltpu.VMEM),
        ),
        out_shape=(
            jax.ShapeDtypeStruct(share_rows.shape, jnp.float32),
            jax.ShapeDtypeStruct((height, rank_size), jnp.bfloat16),
            jax.ShapeDtypeStruct((1, rank_size), jnp.float32),
        ),
        scratch_shapes=[
            pltpu.VMEM((rank_size, rank_size), jnp.float32),
            pltpu.VMEM((rank_size, 2 * rank_size), jnp.float32),
            pltpu.VMEM((rank_size, rank_size), jnp.float32),
            pltpu.VMEM((height, rank_size), jnp.bfloat16),
            pltpu.VMEM((height, rank_size), jnp.bfloat16),
            pltpu.SemaphoreType.DMA,
            pltpu.SemaphoreType.DMA((parts,)),
        ],
        compiler_params=pltpu.CompilerParams(vmem_limit_bytes=32 * 2**20),
    )(packed, prior_sv.reshape(1, rank_size), share_rows, basis_rows)


def mass_pieces_kernel(slots, counts_ref, scale_ref, ids_ref, pieces_ref, mass):
    step = pl.program_id(0)
    width = counts_ref.shape[0] // slots
    docs = counts_ref.shape[1]
    doc_blocks = scale_ref.shape[0]
    marker = (
        lax.broadcasted_iota(jnp.int32, (16, docs), 1) // (docs // doc_blocks)
        == lax.broadcasted_iota(jnp.int32, (16, docs), 0)
    ).astype(jnp.bfloat16)
    for slot in range(slots):
        block = counts_ref[slot * width : (slot + 1) * width, :]
        sums = lax.dot_general(
            marker, block, (((1,), (1,)), ((), ())), preferred_element_type=jnp.float32
        )
        place = step * slots + slot
        total = sums[0:1] * scale_ref[0, place]
        for j in range(1, doc_blocks):
            total = total + sums[j : j + 1] * scale_ref[j, place]
        mass[pl.ds(place, 1), :] = total

    @pl.when(step == pl.num_programs(0) - 1)
    def _():
        stored = mass.shape[0]
        even = jnp.concatenate([mass[q : q + 1, :] for q in range(0, stored, 2)], axis=0)
        odd = jnp.concatenate([mass[q : q + 1, :] for q in range(1, stored, 2)], axis=0)
        half = LANES // 2
        lower = lax.broadcasted_iota(jnp.int32, even.shape, 1) < half
        near = jnp.where(lower, even, pltpu.roll(odd, half, 1))
        far = jnp.where(lower, pltpu.roll(even, half, 1), odd)
        ids = jnp.concatenate(
            [ids_ref[...].astype(jnp.float32), jnp.full((1, LANES - stored), -1.0, jnp.float32)], axis=1
        )
        period = jnp.concatenate([near, ids, far, ids] * 4, axis=0)
        rows = period.shape[0]
        for part in range(pieces_ref.shape[0] // rows):
            pieces_ref[part * rows : (part + 1) * rows, :] = period


def mass_pieces(counts, scales, block_ids, doc_count):
    height, docs = counts.shape
    stored = block_ids.shape[0]
    steps = 2
    return pl.pallas_call(
        functools.partial(mass_pieces_kernel, stored // steps),
        grid=(steps,),
        in_specs=[
            pl.BlockSpec((height // steps, docs), lambda i: (i, 0)),
            pl.BlockSpec(memory_space=pltpu.SMEM),
            pl.BlockSpec((1, stored), lambda i: (0, 0)),
        ],
        out_specs=pl.BlockSpec((doc_count * (stored // 2 + 1), LANES), lambda i: (0, 0)),
        out_shape=jax.ShapeDtypeStruct((doc_count * (stored // 2 + 1), LANES), jnp.float32),
        scratch_shapes=[pltpu.VMEM((stored, height // stored), jnp.float32)],
        compiler_params=pltpu.CompilerParams(vmem_limit_bytes=56 * 2**20),
    )(counts, scales.T, block_ids.reshape(1, stored))


def turn_kernel(after_ref, counts_ref, turned_ref):
    turned_ref[...] = counts_ref[...].T


def turn(counts, after):
    height, docs = counts.shape
    steps = 4
    return pl.pallas_call(
        turn_kernel,
        grid=(steps,),
        in_specs=[
            pl.BlockSpec(memory_space=pl.ANY),
            pl.BlockSpec((height // steps, docs), lambda i: (i, 0)),
        ],
        out_specs=pl.BlockSpec((docs, height // steps), lambda i: (0, i)),
        out_shape=jax.ShapeDtypeStruct((docs, height), counts.dtype),
        compiler_params=pltpu.CompilerParams(vmem_limit_bytes=56 * 2**20),
        cost_estimate=pl.CostEstimate(
            flops=0, bytes_accessed=4 * height * docs, transcendentals=0
        ),
    )(after, counts)


def find_masses_kernel(stored, place_ref, incoming_ref, before_ref, keep_ref, send_ref):
    piece = stored // 2 + 1
    batches = incoming_ref.shape[0] // piece
    half = LANES // 2
    chip, core = place_ref[0], place_ref[1]
    ids = incoming_ref[pl.ds(piece - 1, batches, stride=piece), :].T[:stored]
    batch = lax.broadcasted_iota(jnp.int32, ids.shape, 1)
    pair = [
        jnp.sum(jnp.where(batch == 2 * chip + side, ids, 0.0), axis=1, keepdims=True)
        for side in (0, 1)
    ]
    wanted = jnp.broadcast_to(jnp.concatenate(pair, axis=0), (2 * stored, batches))
    matches, parts = [], [[], [], []]
    for row in range(piece - 1):
        masses = incoming_ref[pl.ds(row, batches, stride=piece), :]
        high = masses.astype(jnp.bfloat16)
        rest = masses - high.astype(jnp.float32)
        low = rest.astype(jnp.bfloat16)
        last = (rest - low.astype(jnp.float32)).astype(jnp.bfloat16)
        for part, value in zip(parts, (high, low, last)):
            part.append(value)
        match = [
            jnp.where(wanted == ids[2 * row + slot : 2 * row + slot + 1], 1.0, 0.0)
            for slot in range(2)
        ]
        matches.append(jnp.concatenate(match, axis=0).astype(jnp.bfloat16))
    matches = jnp.concatenate(matches, axis=1)
    found = 0.0
    for part in parts:
        found = found + jnp.dot(
            matches, jnp.concatenate(part, axis=0), preferred_element_type=jnp.float32
        )
    masses = found[: 2 * stored, :half] + found[2 * stored :, half:]
    mine = core == 0
    keep_ref[...] = jnp.where(mine, masses[:stored], masses[stored:])
    send_ref[...] = jnp.where(mine, masses[stored:], masses[:stored])


def find_masses(incoming, before, chip, core, stored):
    shape = jax.ShapeDtypeStruct((stored, LANES // 2), jnp.float32)
    return pl.pallas_call(
        functools.partial(find_masses_kernel, stored),
        in_specs=[
            pl.BlockSpec(memory_space=pltpu.SMEM),
            pl.BlockSpec(memory_space=pltpu.VMEM),
            pl.BlockSpec(memory_space=pl.ANY),
        ],
        out_specs=(pl.BlockSpec(memory_space=pltpu.VMEM), pl.BlockSpec(memory_space=pltpu.VMEM)),
        out_shape=(shape, shape),
        compiler_params=pltpu.CompilerParams(vmem_limit_bytes=6 * 2**20),
    )(jnp.stack([chip, core]).astype(jnp.int32), incoming, before)


def project_kernel(
    total_docs, core_ref, keep_ref, come_ref, scale_ref, prior_ref, turned_ref, partial_ref, basis
):
    stored = keep_ref.shape[0]
    doc_blocks = scale_ref.shape[0]
    height = prior_ref.shape[0]
    width = height // stored
    docs = partial_ref.shape[0] // doc_blocks
    mine, other = keep_ref[...], come_ref[...]
    first = core_ref[0] == 0
    term_mass = jnp.concatenate(
        [jnp.where(first, mine, other), jnp.where(first, other, mine)], axis=1
    )
    weight = jnp.log(1.0 + total_docs / (1.0 + term_mass))
    spare = jnp.zeros((LANES - stored, LANES), jnp.float32)
    turned_weight = jnp.concatenate([weight, spare], axis=0).T[:, :stored]
    columns = [turned_weight * scale_ref[j : j + 1, :] / math.sqrt(TERMS) for j in range(doc_blocks)]
    for block in range(stored):
        span = slice(block * width, (block + 1) * width)
        prior = prior_ref[span, :].astype(jnp.float32)
        for j in range(doc_blocks):
            basis[j, span, :] = (prior * columns[j][:, block : block + 1]).astype(jnp.bfloat16)
    for j in range(doc_blocks):
        partial_ref[j * docs : (j + 1) * docs, :] = jnp.dot(
            turned_ref[j * docs : (j + 1) * docs, :], basis[j], preferred_element_type=jnp.float32
        )


def project(core, keep, come, scales, prior, turned, total_docs):
    height, rank_size = prior.shape
    docs = turned.shape[0]
    doc_blocks = scales.shape[1]
    vmem = pl.BlockSpec(memory_space=pltpu.VMEM)
    return pl.pallas_call(
        functools.partial(project_kernel, total_docs),
        in_specs=[pl.BlockSpec(memory_space=pltpu.SMEM)] + [vmem] * 5,
        out_specs=vmem,
        out_shape=jax.ShapeDtypeStruct((docs, rank_size), jnp.float32),
        scratch_shapes=[pltpu.VMEM((doc_blocks, height, rank_size), jnp.bfloat16)],
        compiler_params=pltpu.CompilerParams(vmem_limit_bytes=32 * 2**20),
    )(core.reshape(1).astype(jnp.int32), keep, come, scales.T, prior, turned)


def shards(tf_blocks, block_scale, term_blocks, prior_rows, prior_sv):
    counts = tf_blocks[0]
    scales = block_scale[0]
    block_ids = term_blocks[0]
    basis_rows = prior_rows[0]
    stored_blocks = block_ids.shape[0]
    batch_docs = counts.shape[1]
    rank_size = basis_rows.shape[1]
    planes, lines = lax.axis_size("z"), lax.axis_size("y")
    doc_count = planes * lines * lax.axis_size("core")
    term_count = lax.axis_size("term")
    total_docs = batch_docs * doc_count
    share_docs = batch_docs // term_count
    pieces = mass_pieces(counts, scales, block_ids, doc_count)
    incoming = all_to_all(pieces.reshape(doc_count, 1, -1), ("z", "y", "core"))
    turned = turn(counts, pieces[:8])
    chip = lax.axis_index("z") * lines + lax.axis_index("y")
    core = lax.axis_index("core")
    keep, send = find_masses(incoming.reshape(-1, LANES), turned[:16, :LANES], chip, core, stored_blocks)
    come = swap_cores(send)
    partial = project(core, keep, come, scales, basis_rows, turned, total_docs)
    partial = partial.reshape(term_count, share_docs, rank_size)
    share_rows, packed = own_gram(all_to_all(partial, "term"), total_docs)
    plane = ("y", "term")
    across = ("z", "core")
    plane_count = lines * term_count
    plane_gram = jnp.sum(all_to_all(packed.reshape(plane_count, 1, -1), plane), axis=0)
    piece_gram = jnp.sum(all_to_all(repeat(plane_gram, doc_count // lines), across), axis=0)
    packed = all_to_all(repeat(piece_gram, plane_count), plane).reshape(-1, LANES)
    doc_coords, new_rows, singular = finish(packed, prior_sv, share_rows, basis_rows)
    return (doc_coords, new_rows[None], singular.reshape(rank_size))


def solution(mesh):
    planes = lines = 8
    named = Mesh(
        mesh.devices.reshape(planes, lines, -1, mesh.shape["term"]), ("z", "y", "core", "term")
    )
    doc = ("z", "y", "core")
    in_specs = (
        P(doc, "term", None),
        P(doc, "term", None),
        P(doc, "term"),
        P(doc, "term", None),
        P(),
    )
    out_specs = (P(doc + ("term",), None), P(doc, "term", None), P())
    return jax.shard_map(shards, mesh=named, in_specs=in_specs, out_specs=out_specs, check_vma=False)
```
